256 devices in a mesh: sec: 8 (over y, core), xy: 32 (over z, x).
Axes of the slice: x: 4, y: 4, z: 8, core: 2. Of those that a mesh axis runs over, the one named last changes fastest.
Arguments:
- sections_img: bfloat16 [8, 8192, 2048], P('sec', 'xy'), may hold values from -8 to 8
- missing: int32 [8], replicated, may hold values 0 or 1
- patch_anchor: int32 [2, 32, 8], P(None, 'xy', 'sec'), may hold values from -64 to 64
- block_valid: int32 [32, 8], P('xy', 'sec'), may hold values 0 or 1
Outputs:
- flow: float32 [2, 2, 8, 32, 8], P(None, None, None, 'xy', 'sec')
The draws below stay inside these ranges and needn't reach their ends.
All inputs are finite; a program needn't handle non-finite values. No bound on the sum of `block_valid` on one device may be relied on, other than what follows from the above.
Results may differ from the reference program's by a relative error of at most 0.004.
Values may be sent and summed in bfloat16 or wider, within the bound.
A program may use at most 64 MiB of HBM per device.

```python
import math
import jax
import jax.numpy as jnp
from jax import lax

PATCH = 256
MARGIN = 64
BLOCK_ROWS = 256
BLOCK_COLS = 256
SECTIONS = 8
ROW_BLOCKS = 32
COL_BLOCKS = 8
IMG_ROWS = 8192
IMG_COLS = 2048


def spread_blocks(field, factor):
    blocked = field.reshape(ROW_BLOCKS, BLOCK_ROWS, COL_BLOCKS, BLOCK_COLS)
    return (blocked * factor[:, None, :, None]).reshape(IMG_ROWS, IMG_COLS)


def draw_sections_img(key, part):
    key = jax.random.fold_in(key, 11)
    fine_key, middle_key, coarse_key, blend_key, step_key, half_key, noise_key = jax.random.split(key, 7)
    middle_shape = (IMG_ROWS // 4, IMG_COLS // 4)
    coarse_shape = (IMG_ROWS // 16, IMG_COLS // 16)
    fine = jax.random.normal(fine_key, (IMG_ROWS, IMG_COLS), jnp.float32)
    middle = jax.random.normal(middle_key, middle_shape, jnp.float32)
    coarse = jax.random.normal(coarse_key, coarse_shape, jnp.float32)
    middle_full = jnp.repeat(jnp.repeat(middle, 4, axis=0), 4, axis=1)
    coarse_full = jnp.repeat(jnp.repeat(coarse, 16, axis=0), 16, axis=1)
    blend = jax.random.uniform(blend_key, (3, ROW_BLOCKS, COL_BLOCKS), jnp.float32, 0.2, 1.2)
    texture = spread_blocks(fine, blend[0]) + spread_blocks(middle_full, blend[1]) + spread_blocks(coarse_full, blend[2])
    step_most = PATCH // 12
    shift_most = 3 * PATCH // 16
    steps = jax.random.randint(step_key, (SECTIONS, 2, ROW_BLOCKS, COL_BLOCKS), -step_most, step_most + 1, dtype=jnp.int32)
    shifts = jnp.clip(jnp.cumsum(steps, axis=0), -shift_most, shift_most).astype(jnp.int32)
    halves = jax.random.randint(half_key, (SECTIONS, 2, ROW_BLOCKS, COL_BLOCKS), 0, 2, dtype=jnp.int32)
    row_index = jnp.arange(IMG_ROWS, dtype=jnp.int32)
    col_index = jnp.arange(IMG_COLS, dtype=jnp.int32)
    row_owner = (row_index // BLOCK_ROWS)[:, None]
    col_owner = (col_index // BLOCK_COLS)[None, :]

    def one_section(inputs):
        shift_now, half_now, section = inputs
        down = shift_now[0][row_owner, col_owner]
        across = shift_now[1][row_owner, col_owner]
        half_down = half_now[0][row_owner, col_owner]
        half_across = half_now[1][row_owner, col_owner]
        rows_at = (row_index[:, None] + down) % IMG_ROWS
        cols_at = (col_index[None, :] + across) % IMG_COLS
        rows_next = (rows_at + half_down) % IMG_ROWS
        cols_next = (cols_at + half_across) % IMG_COLS
        corner_a = texture[rows_at, cols_at]
        corner_b = texture[rows_at, cols_next]
        corner_c = texture[rows_next, cols_at]
        corner_d = texture[rows_next, cols_next]
        value = (corner_a + corner_b + (corner_c + corner_d)) * 0.25
        noise = jax.random.normal(jax.random.fold_in(noise_key, section), (IMG_ROWS, IMG_COLS), jnp.float32)
        return jnp.clip(value + 0.3 * noise, -8.0, 8.0).astype(jnp.bfloat16)
    return lax.map(one_section, (shifts, halves, jnp.arange(SECTIONS, dtype=jnp.int32)))


def draw_patch_anchor(key, part):
    key = jax.random.fold_in(key, 23)
    anchor = jax.random.randint(key, (2, ROW_BLOCKS, COL_BLOCKS), -MARGIN, MARGIN + 1, dtype=jnp.int32)
    anchor = anchor.at[0, 0, 0].set(-MARGIN).at[0, ROW_BLOCKS - 1, 0].set(MARGIN)
    anchor = anchor.at[1, 0, 0].set(MARGIN).at[1, 0, COL_BLOCKS - 1].set(-MARGIN)
    return anchor


def touch_ends(entries, own_key, least, high):
    longest = entries.shape.index(max(entries.shape))
    spots = []
    for shift in (0, 1):
        where = [jax.random.randint(jax.random.fold_in(own_key, axis), (), 0, length) for axis, length in enumerate(entries.shape)]
        where[longest] = (where[longest] + shift) % entries.shape[longest]
        spots.append(tuple(where))
    return entries.at[spots[0]].set(least).at[spots[1]].set(high)


def setup_inputs(seed: int = 0) -> dict:
    splits = jax.random.split(jax.random.key(seed), 5)
    return {
        "sections_img": draw_sections_img(jax.random.fold_in(splits[4], 71), 0),
        "missing": touch_ends((jax.random.randint(splits[1], (SECTIONS,), 0, 4) < 1).astype(jnp.int32), jax.random.fold_in(splits[1], 1), 0, 1),
        "patch_anchor": draw_patch_anchor(jax.random.fold_in(splits[4], 71), 0),
        "block_valid": touch_ends((jax.random.randint(splits[3], (ROW_BLOCKS, COL_BLOCKS), 0, 4) < 3).astype(jnp.int32), jax.random.fold_in(splits[3], 1), 0, 1),
    }


BETA = 30.0
SHIFT_UNIT = 8.0

def dft_tables(length):
    index = jnp.arange(length, dtype=jnp.int32)
    product = index[:, None] * index[None, :] % length
    phase = product.astype(jnp.float32) * (2.0 * math.pi / length)
    return (jnp.cos(phase).astype(jnp.bfloat16), jnp.sin(phase).astype(jnp.bfloat16))

def matmul(form, left, right):
    return jnp.einsum(form, left.astype(jnp.float32), right.astype(jnp.float32), precision=lax.Precision.HIGHEST)

def normalize(patch):
    values = patch.astype(jnp.float32)
    centred = values - lax.optimization_barrier(jnp.mean(values, axis=(1, 2), keepdims=True))
    spread = lax.optimization_barrier(jnp.mean(centred * centred, axis=(1, 2), keepdims=True))
    return (centred * lax.rsqrt(spread + 1e-05)).astype(jnp.bfloat16)

def forward(normed, cosine, sine):
    first_re = matmul('npq,qk->npk', normed, cosine).astype(jnp.bfloat16)
    first_im = (-matmul('npq,qk->npk', normed, sine)).astype(jnp.bfloat16)
    spec_re = (matmul('jp,npk->njk', cosine, first_re) + matmul('jp,npk->njk', sine, first_im)).astype(jnp.bfloat16)
    spec_im = (matmul('jp,npk->njk', cosine, first_im) - matmul('jp,npk->njk', sine, first_re)).astype(jnp.bfloat16)
    return (spec_re, spec_im)

def correlate(left_re, left_im, right_re, right_im, cosine, sine):
    a_re = left_re.astype(jnp.float32)
    a_im = left_im.astype(jnp.float32)
    b_re = right_re.astype(jnp.float32)
    b_im = right_im.astype(jnp.float32)
    cross_re = (a_re * b_re + a_im * b_im).astype(jnp.bfloat16)
    cross_im = (a_re * b_im - a_im * b_re).astype(jnp.bfloat16)
    half_re = (matmul('npq,qk->npk', cross_re, cosine) - matmul('npq,qk->npk', cross_im, sine)).astype(jnp.bfloat16)
    half_im = (matmul('npq,qk->npk', cross_re, sine) + matmul('npq,qk->npk', cross_im, cosine)).astype(jnp.bfloat16)
    full = matmul('jp,npk->njk', cosine, half_re) - matmul('jp,npk->njk', sine, half_im)
    return full / float(PATCH) ** 4

def soft_shift(corr):
    length = corr.shape[1]
    index = jnp.arange(length, dtype=jnp.int32)
    signed = jnp.where(index < length // 2, index, index - length).astype(jnp.float32)
    weight = jnp.exp(BETA * corr)
    total = lax.optimization_barrier(jnp.sum(weight, axis=(1, 2)))
    shift_row = lax.optimization_barrier(jnp.sum(weight * signed[None, :, None], axis=(1, 2))) / total / SHIFT_UNIT
    shift_col = lax.optimization_barrier(jnp.sum(weight * signed[None, None, :], axis=(1, 2))) / total / SHIFT_UNIT
    return (shift_row, shift_col)

def block_flow(patch, present, cosine, sine):
    normed = normalize(patch)
    spec_re, spec_im = forward(normed, cosine, sine)
    per_lag = []
    for lag in (1, 2):
        corr = correlate(spec_re[:-lag], spec_im[:-lag], spec_re[lag:], spec_im[lag:], cosine, sine)
        shift_row, shift_col = soft_shift(corr)
        keep = present[:-lag] * present[lag:]
        filler = jnp.zeros((lag,), jnp.float32)
        per_lag.append(jnp.stack([jnp.concatenate([shift_row * keep, filler]), jnp.concatenate([shift_col * keep, filler])]))
    return jnp.stack(per_lag, axis=1)

def reference(sections_img, missing, patch_anchor, block_valid):
    cosine, sine = dft_tables(PATCH)
    padded = jnp.pad(sections_img, ((0, 0), (MARGIN, MARGIN), (MARGIN, MARGIN)))
    present = (1 - missing).astype(jnp.float32)

    def one_block(index):
        row_block = index // COL_BLOCKS
        col_block = index % COL_BLOCKS
        top = (row_block * BLOCK_ROWS + MARGIN + patch_anchor[0, row_block, col_block]).astype(jnp.int32)
        left = (col_block * BLOCK_COLS + MARGIN + patch_anchor[1, row_block, col_block]).astype(jnp.int32)
        start = jnp.zeros((), jnp.int32)
        patch = lax.dynamic_slice(padded, (start, top, left), (SECTIONS, PATCH, PATCH))
        flows = block_flow(patch, present, cosine, sine)
        return flows * block_valid[row_block, col_block].astype(jnp.float32)
    stacked = lax.map(one_block, jnp.arange(ROW_BLOCKS * COL_BLOCKS, dtype=jnp.int32))
    stacked = stacked.reshape(ROW_BLOCKS, COL_BLOCKS, 2, 2, SECTIONS)
    return jnp.transpose(stacked, (2, 3, 4, 0, 1))
```

```python
import functools
import math

import jax
import jax.numpy as jnp
import numpy as np
from jax import lax
from jax.experimental import pallas as pl
from jax.experimental.pallas import tpu as pltpu
from jax.sharding import PartitionSpec as P

PATCH = 256
HALF = PATCH // 2
MARGIN = 64
LANES = 128
EXTRA = 16
BETA = 30.0
SHIFT_UNIT = 8.0
MESH = pl.DeviceIdType.MESH


def tables():
    index = np.arange(PATCH)
    phase = (index[:, None] * index[None, :] % PATCH).astype(np.float32) * np.float32(2.0 * math.pi / PATCH)
    cosine, sine = np.cos(phase), np.sin(phase)
    alternating = np.where(index % 2 == 0, 1.0, -1.0).astype(np.float32)
    analysis = np.concatenate([cosine[:HALF], -sine[:HALF]], axis=0)
    analysis[HALF] = alternating
    synthesis = np.concatenate([2.0 * cosine[:, :HALF], -2.0 * sine[:, :HALF]], axis=1)
    synthesis[:, 0] = 1.0
    synthesis[:, HALF] = alternating
    return np.stack([cosine, sine, analysis, synthesis]).astype(jnp.bfloat16)


def dot(left, right):
    return jnp.dot(left, right, preferred_element_type=jnp.float32)


def kernel(
    sec_count,
    row_count,
    x_ref,
    anchor_ref,
    table_ref,
    out_ref,
    own,
    above,
    below,
    table,
    anchors,
    patch,
    send,
    spec,
    stat_plain,
    stat_row,
    local_sem,
    halo_send,
    halo_recv,
    anchor_send,
    anchor_recv,
    spec_send,
    spec_recv,
):
    a = lax.axis_index("sec")
    r = lax.axis_index("xy")
    row_next = lax.rem(r + 1, row_count)
    row_before = lax.rem(r + row_count - 1, row_count)
    wide = sec_count * PATCH

    local_own = pltpu.make_async_copy(x_ref.at[0], own.at[:, pl.ds(LANES, wide)], local_sem.at[0])
    local_table = pltpu.make_async_copy(table_ref, table, local_sem.at[1])
    local_own.start()
    local_table.start()

    barrier = pltpu.get_barrier_semaphore()
    for other in (row_next, row_before):
        pl.semaphore_signal(barrier, inc=1, device_id=(a, other), device_id_type=MESH)
    for step in range(1, sec_count):
        pl.semaphore_signal(barrier, inc=1, device_id=(lax.rem(a + step, sec_count), r), device_id_type=MESH)

    me_row = jnp.full((1, LANES), anchor_ref[0, 0, 0], jnp.float32)
    me_col = jnp.full((1, LANES), anchor_ref[1, 0, 0], jnp.float32)
    anchors[a] = jnp.concatenate([me_row, me_col, jnp.zeros((6, LANES), jnp.float32)], axis=0)
    for ref in (own, above, below):
        rows = ref.shape[0]
        ref[:, 0:LANES] = jnp.zeros((rows, LANES), jnp.bfloat16)
        ref[:, LANES + wide :] = jnp.zeros((rows, LANES), jnp.bfloat16)
    stat_plain[...] = jnp.ones_like(stat_plain)
    stat_row[...] = jnp.zeros_like(stat_row)

    pl.semaphore_wait(barrier, sec_count + 1)

    def anchor_copy(step):
        to = lax.rem(a + step, sec_count)
        return pltpu.make_async_remote_copy(
            src_ref=anchors.at[a],
            dst_ref=anchors.at[a],
            send_sem=anchor_send.at[step],
            recv_sem=anchor_recv.at[step],
            device_id=(to, r),
            device_id_type=MESH,
        )

    first = lax.rem(a + 2, sec_count)

    def halo_copy(step, side):
        at = lax.rem(first + step + sec_count - 1, sec_count)
        source = pl.ds(pl.multiple_of(at * PATCH, PATCH), PATCH)
        target = pl.ds(pl.multiple_of(at * PATCH + LANES, LANES), PATCH)
        rows, ref, to = ((PATCH - MARGIN, above, row_next), (0, below, row_before))[side]
        return pltpu.make_async_remote_copy(
            src_ref=x_ref.at[0, pl.ds(rows, MARGIN), source],
            dst_ref=ref.at[:, target],
            send_sem=halo_send.at[side, step],
            recv_sem=halo_recv.at[side, step],
            device_id=(a, to),
            device_id_type=MESH,
        )

    for step in range(1, sec_count):
        anchor_copy(step).start()
    for step in range(sec_count):
        for side in (0, 1):
            halo_copy(step, side).start()

    local_own.wait()
    local_table.wait()
    for step in range(1, sec_count):
        anchor_copy(step).wait_recv()

    def spec_copy(step):
        to = lax.rem(first + step, sec_count)
        return pltpu.make_async_remote_copy(
            src_ref=send.at[step],
            dst_ref=spec.at[a],
            send_sem=spec_send.at[step],
            recv_sem=spec_recv.at[a],
            device_id=(to, r),
            device_id_type=MESH,
        )

    def wait_halo(step):
        for side in (0, 1):
            halo_copy(step, side).wait_recv()

    wait_halo(0)
    wait_halo(1)
    has_next = jnp.where(r < row_count - 1, 1.0, 0.0)
    has_before = jnp.where(r > 0, 1.0, 0.0)

    def transform(step, _):
        @pl.when(step < sec_count - 2)
        def _():
            wait_halo(step + 2)

        c = lax.rem(first + step, sec_count)
        base = pl.multiple_of(c * PATCH + LANES, LANES)
        shift_row = anchors[c, 0:1, :]
        shift_col = anchors[c, 1:2, :]

        def rows_of(offset):
            lanes = pl.ds(pl.multiple_of(base + offset, LANES), LANES)
            sub = lax.broadcasted_iota(jnp.int32, (MARGIN, LANES), 0).astype(jnp.float32)
            top = jnp.where(
                sub < shift_row,
                below[:, lanes].astype(jnp.float32) * has_next,
                own[0:MARGIN, lanes].astype(jnp.float32),
            )
            middle = own[MARGIN : PATCH - MARGIN, lanes].astype(jnp.float32)
            bottom = jnp.where(
                sub >= shift_row + MARGIN,
                above[:, lanes].astype(jnp.float32) * has_before,
                own[PATCH - MARGIN :, lanes].astype(jnp.float32),
            )
            return jnp.concatenate([top, middle, bottom], axis=0)

        lane = lax.broadcasted_iota(jnp.int32, (PATCH, LANES), 1).astype(jnp.float32)
        left = jnp.where(lane < shift_col, rows_of(PATCH), rows_of(0))
        right = jnp.where(lane >= shift_col + LANES, rows_of(-LANES), rows_of(LANES))
        patch[:, 0:LANES] = left
        patch[:, LANES:] = right
        values = patch[...]
        count = 1.0 / (PATCH * PATCH)
        centred = values - jnp.sum(values) * count
        spread = jnp.sum(centred * centred) * count
        normed = (centred * lax.rsqrt(jnp.full((1, 1), spread + 1e-05, jnp.float32))).astype(jnp.bfloat16)

        rows = dot(table[2], normed).astype(jnp.bfloat16)
        by_cos = dot(rows, table[0])
        by_sin = dot(rows, table[1])
        head = lax.broadcasted_iota(jnp.int32, (HALF, PATCH), 0) == 0
        zero = jnp.zeros((HALF, PATCH), jnp.float32)
        spec_re = by_cos[:HALF] + jnp.where(head, zero, by_sin[HALF:])
        spec_im = jnp.where(head, zero, by_cos[HALF:]) - by_sin[:HALF]
        last_re = jnp.where(head, by_cos[HALF:], zero)[:8]
        last_im = jnp.where(head, -by_sin[HALF:], zero)[:8]
        send[step, 0:HALF, :] = spec_re.astype(jnp.bfloat16)
        send[step, HALF:PATCH, :] = spec_im.astype(jnp.bfloat16)
        send[step, PATCH:, :] = jnp.concatenate([last_re, last_im], axis=0).astype(jnp.bfloat16)

        @pl.when(c != a)
        def _():
            spec_copy(step).start()

        @pl.when(c == a)
        def _():
            spec[a] = send[step]

        return 0

    lax.fori_loop(0, sec_count, transform, 0)

    def arrived(s):
        @pl.when(s != a)
        def _():
            pltpu.make_async_remote_copy(
                src_ref=send.at[0],
                dst_ref=spec.at[s],
                send_sem=spec_send.at[0],
                recv_sem=spec_recv.at[s],
                device_id=(s, r),
                device_id_type=MESH,
            ).wait_recv()

    def cross(s, t):
        a_re = spec[s, 0:HALF, :].astype(jnp.float32)
        a_im = spec[s, HALF:PATCH, :].astype(jnp.float32)
        b_re = spec[t, 0:HALF, :].astype(jnp.float32)
        b_im = spec[t, HALF:PATCH, :].astype(jnp.float32)
        cross_re = a_re * b_re + a_im * b_im
        cross_im = a_re * b_im - a_im * b_re
        e = spec[s, PATCH:, :].astype(jnp.float32)
        f = spec[t, PATCH:, :].astype(jnp.float32)
        last_re = e[:8] * f[:8] + e[8:] * f[8:]
        last_im = e[:8] * f[8:] - e[8:] * f[:8]
        cross_re = jnp.concatenate([cross_re[:8] - last_im, cross_re[8:]], axis=0)
        cross_im = jnp.concatenate([cross_im[:8] + last_re, cross_im[8:]], axis=0)
        return jnp.concatenate([cross_re, cross_im], axis=0).astype(jnp.bfloat16)

    scale = BETA / math.log(2.0) / float(PATCH) ** 4
    group = lax.broadcasted_iota(jnp.int32, (PATCH // 8, 8, PATCH), 0).astype(jnp.float32) * 8.0
    signed_group = jnp.where(group < HALF, group, group - PATCH)

    def correlate(s, t, slot):
        pair = cross(s, t)
        by_cos = dot(pair, table[0])
        by_sin = dot(pair, table[1])
        half_re = by_cos[:HALF] - by_sin[HALF:]
        half_im = by_sin[:HALF] + by_cos[HALF:]
        half = jnp.concatenate([half_re, half_im], axis=0).astype(jnp.bfloat16)
        weight = jnp.exp2(dot(table[3], half) * scale).reshape(PATCH // 8, 8, PATCH)
        stat_plain[slot] = jnp.sum(weight, axis=0)
        stat_row[slot] = jnp.sum(weight * signed_group, axis=0)

    arrived(0)

    def pairs(t, _):
        arrived(t)
        correlate(t - 1, t, t - 1)
        back = jnp.maximum(t - 2, 0)
        correlate(back, t, jnp.where(t >= 2, sec_count + back, 2 * sec_count - 1))
        return 0

    lax.fori_loop(1, sec_count, pairs, 0)

    plain = stat_plain[...]
    sub = lax.broadcasted_iota(jnp.int32, plain.shape, 1).astype(jnp.float32)
    by_row = jnp.sum(stat_row[...] + sub * plain, axis=1)
    plain = jnp.sum(plain, axis=1)
    column = lax.broadcasted_iota(jnp.int32, plain.shape, 1).astype(jnp.float32)
    signed = jnp.where(column < HALF, column, column - PATCH)
    total = jnp.sum(plain, axis=1, keepdims=True)
    shift_row = jnp.sum(by_row, axis=1, keepdims=True) / total / SHIFT_UNIT
    shift_col = jnp.sum(plain * signed, axis=1, keepdims=True) / total / SHIFT_UNIT
    lane = lax.broadcasted_iota(jnp.int32, out_ref.shape, 1)
    out_ref[...] = jnp.where(lane == 0, shift_row, shift_col)

    for step in range(1, sec_count):
        anchor_copy(step).wait_send()
    for step in range(sec_count):
        for side in (0, 1):
            halo_copy(step, side).wait_send()

    def sent(step, _):
        @pl.when(lax.rem(first + step, sec_count) != a)
        def _():
            spec_copy(step).wait_send()

        return 0

    lax.fori_loop(0, sec_count, sent, 0)


def body(sec_count, row_count, sections_img, missing, patch_anchor, block_valid):
    wide = sec_count * PATCH
    bf16, f32 = jnp.bfloat16, jnp.float32
    dma = pltpu.SemaphoreType.DMA
    shifts = pl.pallas_call(
        functools.partial(kernel, sec_count, row_count),
        out_shape=jax.ShapeDtypeStruct((2 * sec_count, LANES), f32),
        in_specs=[
            pl.BlockSpec(memory_space=pl.ANY),
            pl.BlockSpec(memory_space=pltpu.SMEM),
            pl.BlockSpec(memory_space=pl.ANY),
        ],
        out_specs=pl.BlockSpec(memory_space=pltpu.VMEM),
        scratch_shapes=[
            pltpu.VMEM((PATCH, wide + 2 * LANES), bf16),
            pltpu.VMEM((MARGIN, wide + 2 * LANES), bf16),
            pltpu.VMEM((MARGIN, wide + 2 * LANES), bf16),
            pltpu.VMEM((4, PATCH, PATCH), bf16),
            pltpu.VMEM((sec_count, 8, LANES), f32),
            pltpu.VMEM((PATCH, PATCH), f32),
            pltpu.VMEM((sec_count, PATCH + EXTRA, PATCH), bf16),
            pltpu.VMEM((sec_count, PATCH + EXTRA, PATCH), bf16),
            pltpu.VMEM((2 * sec_count, 8, PATCH), f32),
            pltpu.VMEM((2 * sec_count, 8, PATCH), f32),
            dma((2,)),
            dma((2, sec_count)),
            dma((2, sec_count)),
            dma((sec_count,)),
            dma((sec_count,)),
            dma((sec_count,)),
            dma((sec_count,)),
        ],
        compiler_params=pltpu.CompilerParams(
            collective_id=0, has_side_effects=True, vmem_limit_bytes=40 * 2**20
        ),
        name="flow",
    )(sections_img, patch_anchor, jnp.asarray(tables()))
    present = (1 - missing).astype(f32)
    valid = block_valid[0, 0].astype(f32)
    moved = jnp.transpose(shifts[:, :2].reshape(2, sec_count, 2), (2, 0, 1))
    keep = []
    for lag in (1, 2):
        both = present[:-lag] * present[lag:] * valid
        keep.append(jnp.concatenate([both, jnp.zeros((lag,), f32)]))
    return (moved * jnp.stack(keep)[None])[:, :, :, None, None]


def solution(mesh):
    placed = (P("sec", "xy", None), P(), P(None, "xy", "sec"), P("xy", "sec"))
    return jax.shard_map(
        functools.partial(body, mesh.shape["sec"], mesh.shape["xy"]),
        mesh=mesh,
        in_specs=placed,
        out_specs=P(None, None, None, "xy", "sec"),
        check_vma=False,
    )
```

```python
import functools
import math

import jax
import jax.numpy as jnp
import numpy as np
from jax import lax
from jax.experimental import pallas as pl
from jax.experimental.pallas import tpu as pltpu
from jax.sharding import PartitionSpec as P

PATCH = 256
HALF = PATCH // 2
MARGIN = 64
LANES = 128
EXTRA = 16
SECTIONS = 8
CHIPS = 4
BETA = 30.0
SHIFT_UNIT = 8.0
MESH = pl.DeviceIdType.MESH


def tables():
    index = np.arange(PATCH)
    phase = (index[:, None] * index[None, :] % PATCH).astype(np.float32) * np.float32(2.0 * math.pi / PATCH)
    cosine, sine = np.cos(phase), np.sin(phase)
    alternating = np.where(index % 2 == 0, 1.0, -1.0).astype(np.float32)
    analysis = np.concatenate([cosine[:HALF], -sine[:HALF]], axis=0)
    analysis[HALF] = alternating
    synthesis = np.concatenate([2.0 * cosine[:, :HALF], -2.0 * sine[:, :HALF]], axis=1)
    synthesis[:, 0] = 1.0
    synthesis[:, HALF] = alternating
    return np.stack([cosine, sine, analysis, synthesis]).astype(jnp.bfloat16)


def dot(left, right):
    return jnp.dot(left, right, preferred_element_type=jnp.float32)


def plan():
    orders = []
    for a in range(SECTIONS):
        y, k = a // 2, a % 2
        sign = 1 - 2 * k
        same = [2 * ((y - sign * j) % CHIPS) + k for j in range(CHIPS)]
        peer = [2 * ((y + sign * j) % CHIPS) + 1 - k for j in range(CHIPS)]
        orders.append(same + [peer[1], peer[0], peer[2], peer[3]])
    pairs = range(2 * SECTIONS - 3)
    ready = []
    for order in orders:
        rank = {s: i for i, s in enumerate(order)}
        ready.append(sorted((max(rank[n // 2], rank[n // 2 + 1 + n % 2]), n) for n in pairs))
    steps = [max(entry[i][0] for entry in ready) for i in range(len(pairs))]
    waits = [tuple(order[i] for order in orders) for i in range(SECTIONS)]
    work = [[tuple(entry[i][1] for entry in ready) for i in range(len(pairs)) if steps[i] == q] for q in range(SECTIONS)]
    return waits, work


def pick(values, a):
    if max(values) < 8:
        power = (1 + 7 * (a % 2)) * (1 + 63 * (a // 2 % 2)) * (1 + 4095 * (a // 4))
        return sum(v * 8**i for i, v in enumerate(values)) // power % 8
    return 8 * pick([v // 8 for v in values], a) + pick([v % 8 for v in values], a)


def kernel(
    row_count,
    x_ref,
    anchor_ref,
    missing_ref,
    valid_ref,
    table_ref,
    out_ref,
    anchor,
    missing,
    valid,
    own,
    above,
    below,
    table,
    anchors,
    send,
    passing,
    spec,
    stat_plain,
    stat_row,
    local_sem,
    halo_send,
    halo_recv,
    anchor_send,
    anchor_recv,
    spec_send,
    spec_recv,
    passing_recv,
    passing_send,
):
    a = lax.axis_index("sec")
    r = lax.axis_index("xy")
    y, k = a // 2, a % 2
    sign = 1 - 2 * k
    peer = a + sign
    has_next = 1 - (r + 1) // row_count
    has_before = (r + row_count - 1) // row_count
    wide = SECTIONS * PATCH

    def chip(j):
        return (y + sign * j + 2 * CHIPS) % CHIPS

    def local(source, target, i):
        return pltpu.make_async_copy(source, target, local_sem.at[i])

    def remote(source, target, sent, received, to_a, to_r):
        return pltpu.make_async_remote_copy(
            src_ref=source,
            dst_ref=target,
            send_sem=sent,
            recv_sem=received,
            device_id=(to_a, to_r),
            device_id_type=MESH,
        )

    local_own = local(x_ref.at[0], own.at[:, pl.ds(LANES, wide)], 0)
    local_table = local(table_ref, table, 1)
    small = [local(anchor_ref, anchor, 2), local(missing_ref, missing, 3), local(valid_ref, valid, 4)]
    for copy in small:
        copy.start()
    local_own.start()
    local_table.start()

    barrier = pltpu.get_barrier_semaphore()

    @pl.when(has_next == 1)
    def _():
        pl.semaphore_signal(barrier, inc=1, device_id=(a, r + 1), device_id_type=MESH)

    @pl.when(has_before == 1)
    def _():
        pl.semaphore_signal(barrier, inc=1, device_id=(a, r - 1), device_id_type=MESH)

    for j in (1, 2, 3):
        pl.semaphore_signal(barrier, inc=1, device_id=(2 * chip(j) + k, r), device_id_type=MESH)
    pl.semaphore_signal(barrier, inc=1, device_id=(peer, r), device_id_type=MESH)

    @pl.when(has_next == 0)
    def _():
        below[...] = jnp.zeros_like(below)

    @pl.when(has_before == 0)
    def _():
        above[...] = jnp.zeros_like(above)

    for ref in (own, above, below):
        rows = ref.shape[0]
        ref[:, 0:LANES] = jnp.zeros((rows, LANES), jnp.bfloat16)
        ref[:, LANES + wide :] = jnp.zeros((rows, LANES), jnp.bfloat16)
    stat_plain[...] = jnp.ones_like(stat_plain)
    stat_row[...] = jnp.zeros_like(stat_row)
    for copy in small:
        copy.wait()
    me_row = jnp.full((1, LANES), anchor[0, 0, 0], jnp.float32)
    me_col = jnp.full((1, LANES), anchor[0, 0, 1], jnp.float32)
    anchors[k, y] = jnp.concatenate([me_row, me_col, jnp.zeros((6, LANES), jnp.float32)], axis=0)

    pl.semaphore_wait(barrier, CHIPS + has_next + has_before)

    def anchor_copy(j):
        mine = anchors.at[k, y]
        return remote(mine, mine, anchor_send.at[j], anchor_recv.at[j], 2 * chip(j) + k, r)

    def anchor_share(parity):
        group = anchors.at[parity]
        return remote(group, group, anchor_send.at[0], anchor_recv.at[0], peer, r)

    first = 2 * chip(1) + k

    def halo_copy(m, side):
        at = (first + sign * (m - 1) + SECTIONS) % SECTIONS
        source = pl.ds(pl.multiple_of(at * PATCH, PATCH), PATCH)
        target = pl.ds(pl.multiple_of(at * PATCH + LANES, LANES), PATCH)
        rows, ref, to = ((PATCH - MARGIN, above, r + 1), (0, below, r - 1))[side]
        return remote(
            x_ref.at[0, pl.ds(rows, MARGIN), source],
            ref.at[:, target],
            halo_send.at[side, m],
            halo_recv.at[side, m],
            a,
            to,
        )

    def each_halo(sending, act):
        for side in (0, 1):
            there = has_next if (side == 0) == sending else has_before

            @pl.when(there == 1)
            def _():
                act(side)

    for j in (1, 2, 3):
        anchor_copy(j).start()

    def start_halos(side):
        for m in range(SECTIONS):
            halo_copy(m, side).start()

    each_halo(True, start_halos)

    def wait_halos(steps):
        def wait(side):
            for m in steps:
                halo_copy(m, side).wait_recv()

        each_halo(False, wait)

    local_own.wait()
    local_table.wait()
    for j in (1, 2, 3):
        anchor_copy(j).wait_recv()
    anchor_share(k).start()

    def cut(c, parity):
        base = pl.multiple_of(c * PATCH + LANES, LANES)
        shift_row = anchors[parity, c // 2, 0:1, :]
        shift_col = anchors[parity, c // 2, 1:2, :]
        sub = lax.broadcasted_iota(jnp.int32, (MARGIN, LANES), 0).astype(jnp.float32)
        lane = lax.broadcasted_iota(jnp.int32, (16, LANES), 1).astype(jnp.float32)

        def mask(condition):
            one = jnp.where(condition, 1.0, 0.0)
            return one.astype(jnp.bfloat16), (1.0 - one).astype(jnp.bfloat16)

        from_below, not_below = mask(sub < shift_row)
        from_above, not_above = mask(sub >= shift_row + MARGIN)
        from_right, not_right = mask(lane < shift_col)
        from_left, not_left = mask(lane >= shift_col + LANES)

        def rows_of(offset):
            lanes = pl.ds(pl.multiple_of(base + offset, LANES), LANES)
            top = below[:, lanes] * from_below + own[0:MARGIN, lanes] * not_below
            middle = own[MARGIN : PATCH - MARGIN, lanes]
            bottom = above[:, lanes] * from_above + own[PATCH - MARGIN :, lanes] * not_above
            return jnp.concatenate([top, middle, bottom], axis=0).reshape(PATCH // 16, 16, LANES)

        left = rows_of(PATCH) * from_right[None] + rows_of(0) * not_right[None]
        right = rows_of(-LANES) * from_left[None] + rows_of(LANES) * not_left[None]
        return jnp.concatenate([left.reshape(PATCH, LANES), right.reshape(PATCH, LANES)], axis=1)

    head8 = lax.broadcasted_iota(jnp.int32, (8, PATCH), 0) == 0
    zero8 = jnp.zeros((8, PATCH), jnp.float32)

    def analyse(c, parity):
        values = cut(c, parity)
        rows = dot(table[2], values)
        mean = jnp.sum(rows[0:1, :], axis=1, keepdims=True) * (1.0 / (PATCH * PATCH))
        centred = values.astype(jnp.float32) - mean
        squares = jnp.sum((centred * centred).reshape(PATCH // 8, 8, PATCH), axis=0)
        squares = jnp.sum(jnp.sum(squares, axis=0, keepdims=True), axis=1, keepdims=True)
        scale = lax.rsqrt(squares * (1.0 / (PATCH * PATCH)) + 1e-05)
        top = rows[:8] - jnp.where(head8, mean * float(PATCH), zero8)
        return jnp.concatenate([top, rows[8:]], axis=0).astype(jnp.bfloat16), scale

    def transform(rows, scale, target):
        by_cos = dot(rows, table[0])
        by_sin = dot(rows, table[1])
        real = by_cos[8:HALF] + by_sin[HALF + 8 :]
        imag = by_cos[HALF + 8 :] - by_sin[8:HALF]
        cos_last, sin_last = by_cos[HALF : HALF + 8], by_sin[HALF : HALF + 8]
        real8 = by_cos[:8] + jnp.where(head8, zero8, sin_last)
        imag8 = jnp.where(head8, zero8, cos_last) - by_sin[:8]
        last = jnp.concatenate([jnp.where(head8, cos_last, zero8), jnp.where(head8, -sin_last, zero8)], axis=0)
        whole = jnp.concatenate([real8, real, imag8, imag, last], axis=0)
        target[...] = (whole * scale).astype(jnp.bfloat16)

    def direct(j):
        return remote(send.at[j], spec.at[a], spec_send.at[j], spec_recv.at[a], 2 * chip(j + 1) + k, r)

    def hand(j):
        target = passing.at[j] if j < 3 else spec.at[a]
        received = passing_recv.at[j] if j < 3 else spec_recv.at[a]
        return remote(send.at[3 + j], target, spec_send.at[3 + j], received, peer, r)

    def forward(j):
        to = 2 * chip(-(j + 1)) + k
        return remote(passing.at[j], spec.at[peer], passing_send.at[j], spec_recv.at[peer], to, r)

    for j, steps in enumerate(((0, 1, 2), (3, 4), (5, 6), (7,))):
        wait_halos(steps)
        rows, scale = analyse(2 * chip(j + 1) + k, k)
        transform(rows, scale, send.at[j] if j < 3 else spec.at[a])
        if j < 3:
            direct(j).start()

    anchor_share(1 - k).wait_recv()
    ahead = analyse(2 * chip(1) + 1 - k, 1 - k)
    for j in range(4):
        now = ahead
        if j < 3:
            ahead = analyse(2 * chip(j + 2) + 1 - k, 1 - k)
        transform(*now, send.at[3 + j])
        hand(j).start()
        if j > 0:
            hand(j - 1).wait_recv()
            forward(j - 1).start()

    def cross(s, t):
        def part(section, start, stop):
            return spec[section, start:stop, :].astype(jnp.float32)

        def products(a_re, a_im, b_re, b_im):
            return a_re * b_re + a_im * b_im, a_re * b_im - a_im * b_re

        real, imag = products(part(s, 0, HALF), part(s, HALF, PATCH), part(t, 0, HALF), part(t, HALF, PATCH))
        e, f = part(s, PATCH, PATCH + EXTRA), part(t, PATCH, PATCH + EXTRA)
        last_re, last_im = products(e[:8], e[8:], f[:8], f[8:])
        return jnp.concatenate([real[:8] - last_im, real[8:], imag[:8] + last_re, imag[8:]], axis=0).astype(jnp.bfloat16)

    scale = BETA / math.log(2.0) / float(PATCH) ** 4
    group = lax.broadcasted_iota(jnp.int32, (PATCH // 8, 8, PATCH), 0).astype(jnp.float32) * 8.0
    signed_group = jnp.where(group < HALF, group, group - PATCH)

    def correlate(n):
        s = n // 2
        pair = cross(s, s + 1 + n % 2)
        by_cos = dot(pair, table[0])
        by_sin = dot(pair, table[1])
        half_re = by_cos[:HALF] - by_sin[HALF:]
        half_im = by_sin[:HALF] + by_cos[HALF:]
        half = jnp.concatenate([half_re, half_im], axis=0).astype(jnp.bfloat16)
        weight = jnp.exp2(dot(table[3], half) * scale).reshape(PATCH // 8, 8, PATCH)
        slot = s + SECTIONS * (n % 2)
        stat_plain[slot] = jnp.sum(weight, axis=0)
        stat_row[slot] = jnp.sum(weight * signed_group, axis=0)

    waits, work = plan()
    for q in range(SECTIONS):
        if q > 0:
            s = pick(waits[q], a)
            remote(send.at[0], spec.at[s], spec_send.at[0], spec_recv.at[s], peer, r).wait_recv()
        for entry in work[q]:
            correlate(pick(entry, a))

    plain = stat_plain[...]
    sub = lax.broadcasted_iota(jnp.int32, plain.shape, 1).astype(jnp.float32)
    by_row = jnp.sum(stat_row[...] + sub * plain, axis=1)
    plain = jnp.sum(plain, axis=1)
    column = lax.broadcasted_iota(jnp.int32, plain.shape, 1).astype(jnp.float32)
    signed = jnp.where(column < HALF, column, column - PATCH)
    total = jnp.sum(plain, axis=1, keepdims=True)
    shift_row = jnp.sum(by_row, axis=1, keepdims=True) / total / SHIFT_UNIT
    shift_col = jnp.sum(plain * signed, axis=1, keepdims=True) / total / SHIFT_UNIT
    lane = lax.broadcasted_iota(jnp.int32, (SECTIONS, LANES), 1)
    section = lax.broadcasted_iota(jnp.int32, (SECTIONS, LANES), 0)
    lanes = lax.broadcasted_iota(jnp.int32, (1, LANES), 1)
    for lag in (1, 2):
        keep = jnp.zeros((1, LANES), jnp.float32)
        for s in range(SECTIONS - lag):
            both = (1 - missing[s]) * (1 - missing[s + lag]) * valid[0, 0]
            keep = jnp.where(lanes == s, both.astype(jnp.float32), keep)
        for axis, shift in enumerate((shift_row, shift_col)):
            part = shift[(lag - 1) * SECTIONS : lag * SECTIONS]
            line = jnp.sum(jnp.where(lane == section, part, 0.0), axis=0, keepdims=True) * keep
            out_ref[axis, lag - 1] = line.reshape(1, 1, LANES)[:, :, :SECTIONS]

    def sent_halos(side):
        for m in range(SECTIONS):
            halo_copy(m, side).wait_send()

    each_halo(True, sent_halos)
    for j in (1, 2, 3):
        anchor_copy(j).wait_send()
        direct(j - 1).wait_send()
        forward(j - 1).wait_send()
    anchor_share(k).wait_send()
    for j in range(4):
        hand(j).wait_send()


def body(row_count, sections_img, missing, patch_anchor, block_valid):
    wide = SECTIONS * PATCH
    bf16, f32, i32 = jnp.bfloat16, jnp.float32, jnp.int32
    dma = pltpu.SemaphoreType.DMA
    flow = pl.pallas_call(
        functools.partial(kernel, row_count),
        out_shape=jax.ShapeDtypeStruct((2, 2, 1, 1, SECTIONS), f32),
        in_specs=[pl.BlockSpec(memory_space=pl.ANY)] * 5,
        out_specs=pl.BlockSpec(memory_space=pltpu.VMEM),
        scratch_shapes=[
            pltpu.SMEM((1, 1, 2), i32),
            pltpu.SMEM((SECTIONS,), i32),
            pltpu.SMEM((1, 1), i32),
            pltpu.VMEM((PATCH, wide + 2 * LANES), bf16),
            pltpu.VMEM((MARGIN, wide + 2 * LANES), bf16),
            pltpu.VMEM((MARGIN, wide + 2 * LANES), bf16),
            pltpu.VMEM((4, PATCH, PATCH), bf16),
            pltpu.VMEM((2, CHIPS, 8, LANES), f32),
            pltpu.VMEM((7, PATCH + EXTRA, PATCH), bf16),
            pltpu.VMEM((3, PATCH + EXTRA, PATCH), bf16),
            pltpu.VMEM((SECTIONS, PATCH + EXTRA, PATCH), bf16),
            pltpu.VMEM((2 * SECTIONS, 8, PATCH), f32),
            pltpu.VMEM((2 * SECTIONS, 8, PATCH), f32),
            dma((5,)),
            dma((2, SECTIONS)),
            dma((2, SECTIONS)),
            dma((CHIPS,)),
            dma((CHIPS,)),
            dma((7,)),
            dma((SECTIONS,)),
            dma((3,)),
            dma((3,)),
        ],
        compiler_params=pltpu.CompilerParams(
            collective_id=0, has_side_effects=True, vmem_limit_bytes=60 * 2**20
        ),
        name="flow",
    )(sections_img, jnp.transpose(patch_anchor, (1, 2, 0)), missing, block_valid, jnp.asarray(tables()))
    return jnp.transpose(flow, (0, 1, 4, 2, 3))


def solution(mesh):
    placed = (P("sec", "xy", None), P(), P(None, "xy", "sec"), P("xy", "sec"))
    return jax.shard_map(
        functools.partial(body, mesh.shape["xy"]),
        mesh=mesh,
        in_specs=placed,
        out_specs=P(None, None, None, "xy", "sec"),
        check_vma=False,
    )
```

```python
import functools
import math

import jax
import jax.numpy as jnp
import numpy as np
from jax import lax
from jax.experimental import pallas as pl
from jax.experimental.pallas import tpu as pltpu
from jax.sharding import PartitionSpec as P

PATCH = 256
HALF = PATCH // 2
MARGIN = 64
LANES = 128
EXTRA = 16
SECTIONS = 8
CHIPS = 4
BATCH = 2
BETA = 30.0
SHIFT_UNIT = 8.0
MESH = pl.DeviceIdType.MESH


def tables():
    index = np.arange(PATCH)
    phase = (index[:, None] * index[None, :] % PATCH).astype(np.float32) * np.float32(2.0 * math.pi / PATCH)
    cosine, sine = np.cos(phase), np.sin(phase)
    alternating = np.where(index % 2 == 0, 1.0, -1.0).astype(np.float32)
    analysis = np.concatenate([cosine[:HALF], -sine[:HALF]], axis=0)
    analysis[HALF] = alternating
    synthesis = np.concatenate([2.0 * cosine[:, :HALF], -2.0 * sine[:, :HALF]], axis=1)
    synthesis[:, 0] = 1.0
    synthesis[:, HALF] = alternating
    return np.stack([cosine, sine, analysis, synthesis]).astype(jnp.bfloat16)


def dot(left, right):
    return jnp.dot(left, right, preferred_element_type=jnp.float32)


def plan():
    orders = []
    for a in range(SECTIONS):
        y, k = a // 2, a % 2
        sign = 1 - 2 * k
        same = [2 * ((y - sign * j) % CHIPS) + k for j in range(CHIPS)]
        peer = [2 * ((y + sign * j) % CHIPS) + 1 - k for j in range(CHIPS)]
        orders.append(same + [peer[1], peer[0], peer[2], peer[3]])
    pairs = range(2 * SECTIONS - 3)
    ready = []
    for order in orders:
        rank = {s: i for i, s in enumerate(order)}
        ready.append(sorted((max(rank[n // 2], rank[n // 2 + 1 + n % 2]), n) for n in pairs))
    steps = [max(entry[i][0] for entry in ready) for i in range(len(pairs))]
    waits = [tuple(order[i] for order in orders) for i in range(SECTIONS)]
    work = [[tuple(entry[i][1] for entry in ready) for i in range(len(pairs)) if steps[i] == q] for q in range(SECTIONS)]
    return waits, work


def pick(values, a):
    if max(values) < 8:
        power = (1 + 7 * (a % 2)) * (1 + 63 * (a // 2 % 2)) * (1 + 4095 * (a // 4))
        return sum(v * 8**i for i, v in enumerate(values)) // power % 8
    return 8 * pick([v // 8 for v in values], a) + pick([v % 8 for v in values], a)


def kernel(
    row_count,
    x_ref,
    anchor_ref,
    missing_ref,
    valid_ref,
    table_ref,
    out_ref,
    anchor,
    missing,
    valid,
    own,
    above,
    below,
    table,
    anchors,
    send,
    passing,
    spec,
    stat_plain,
    stat_row,
    local_sem,
    halo_send,
    halo_recv,
    anchor_send,
    anchor_recv,
    spec_send,
    spec_recv,
    passing_recv,
    passing_send,
):
    a = lax.axis_index("sec")
    r = lax.axis_index("xy")
    y, k = a // 2, a % 2
    sign = 1 - 2 * k
    peer = a + sign
    has_next = 1 - (r + 1) // row_count
    has_before = (r + row_count - 1) // row_count
    wide = SECTIONS * PATCH

    def chip(j):
        return (y + sign * j + 2 * CHIPS) % CHIPS

    def local(source, target, i):
        return pltpu.make_async_copy(source, target, local_sem.at[i])

    def remote(source, target, sent, received, to_a, to_r):
        return pltpu.make_async_remote_copy(
            src_ref=source,
            dst_ref=target,
            send_sem=sent,
            recv_sem=received,
            device_id=(to_a, to_r),
            device_id_type=MESH,
        )

    local_own = local(x_ref.at[0], own.at[:, pl.ds(LANES, wide)], 0)
    local_table = local(table_ref, table, 1)
    small = [local(anchor_ref, anchor, 2), local(missing_ref, missing, 3), local(valid_ref, valid, 4)]
    for copy in small:
        copy.start()
    local_own.start()
    local_table.start()

    barrier = pltpu.get_barrier_semaphore()

    @pl.when(has_next == 1)
    def _():
        pl.semaphore_signal(barrier, inc=1, device_id=(a, r + 1), device_id_type=MESH)

    @pl.when(has_before == 1)
    def _():
        pl.semaphore_signal(barrier, inc=1, device_id=(a, r - 1), device_id_type=MESH)

    for j in (1, -1):
        pl.semaphore_signal(barrier, inc=1, device_id=(2 * chip(j) + k, r), device_id_type=MESH)
    pl.semaphore_signal(barrier, inc=1, device_id=(peer, r), device_id_type=MESH)

    @pl.when(has_next == 0)
    def _():
        below[...] = jnp.zeros_like(below)

    @pl.when(has_before == 0)
    def _():
        above[...] = jnp.zeros_like(above)

    own[:, 0:LANES] = jnp.zeros((PATCH, LANES), jnp.bfloat16)
    own[:, LANES + wide :] = jnp.zeros((PATCH, LANES), jnp.bfloat16)
    stat_plain[...] = jnp.ones_like(stat_plain)
    stat_row[...] = jnp.zeros_like(stat_row)
    for copy in small:
        copy.wait()
    me_row = jnp.full((1, LANES), anchor[0, 0, 0], jnp.float32)
    me_col = jnp.full((1, LANES), anchor[0, 0, 1], jnp.float32)
    anchors[k, y] = jnp.concatenate([me_row, me_col, jnp.zeros((6, LANES), jnp.float32)], axis=0)

    local_own.wait()
    pl.semaphore_wait(barrier, 3 + has_next + has_before)

    def anchor_copy(i):
        moved, to = ((y, 1), (y, -1), (chip(1), -1))[i]
        group = anchors.at[k, moved]
        return remote(group, group, anchor_send.at[i], anchor_recv.at[i], 2 * chip(to) + k, r)

    def anchor_share(parity):
        group = anchors.at[parity]
        return remote(group, group, anchor_send.at[3], anchor_recv.at[3], peer, r)

    def halo_copy(m, side):
        if m < CHIPS:
            columns = pl.ds(pl.multiple_of((2 * chip(m + 1) + k) * PATCH, PATCH), 2 * PATCH)
        else:
            columns = pl.ds(pl.multiple_of((1 - k) * wide, PATCH), PATCH)
        rows, ref, to = ((PATCH - MARGIN, above, r + 1), (0, below, r - 1))[side]
        return remote(
            own.at[pl.ds(rows, MARGIN), columns],
            ref.at[:, columns],
            halo_send.at[side, m],
            halo_recv.at[side, m],
            a,
            to,
        )

    def each_halo(sending, act):
        for side in (0, 1):
            there = has_next if (side == 0) == sending else has_before

            @pl.when(there == 1)
            def _():
                act(side)

    anchor_copy(1).start()
    anchor_copy(0).start()

    def start_halo(m):
        each_halo(True, lambda side: halo_copy(m, side).start())

    def wait_halo(m):
        each_halo(False, lambda side: halo_copy(m, side).wait_recv())

    for m in range(CHIPS + 1):
        start_halo(m)

    anchor_copy(1).wait_recv()
    anchor_copy(2).start()
    local_table.wait()

    def cut(c, parity):
        base = pl.multiple_of(c * PATCH + LANES, LANES)
        shift_row = anchors[parity, c // 2, 0:1, :]
        shift_col = anchors[parity, c // 2, 1:2, :]
        sub = lax.broadcasted_iota(jnp.int32, (MARGIN, LANES), 0).astype(jnp.float32)
        lane = lax.broadcasted_iota(jnp.int32, (16, LANES), 1).astype(jnp.float32)

        def mask(condition):
            one = jnp.where(condition, 1.0, 0.0)
            return one.astype(jnp.bfloat16), (1.0 - one).astype(jnp.bfloat16)

        from_below, not_below = mask(sub < shift_row)
        from_above, not_above = mask(sub >= shift_row + MARGIN)
        from_right, not_right = mask(lane < shift_col)
        from_left, not_left = mask(lane >= shift_col + LANES)

        def rows_of(offset):
            lanes = pl.ds(pl.multiple_of(base + offset, LANES), LANES)
            top = below[:, lanes] * from_below + own[0:MARGIN, lanes] * not_below
            middle = own[MARGIN : PATCH - MARGIN, lanes]
            bottom = above[:, lanes] * from_above + own[PATCH - MARGIN :, lanes] * not_above
            return jnp.concatenate([top, middle, bottom], axis=0).reshape(PATCH // 16, 16, LANES)

        left = rows_of(PATCH) * from_right[None] + rows_of(0) * not_right[None]
        right = rows_of(-LANES) * from_left[None] + rows_of(LANES) * not_left[None]
        return jnp.concatenate([left.reshape(PATCH, LANES), right.reshape(PATCH, LANES)], axis=1)

    head8 = lax.broadcasted_iota(jnp.int32, (8, PATCH), 0) == 0
    zero8 = jnp.zeros((8, PATCH), jnp.float32)

    def analyse(c, parity):
        values = cut(c, parity)
        rows = dot(table[2], values)
        mean = jnp.sum(rows[0:1, :], axis=1, keepdims=True) * (1.0 / (PATCH * PATCH))
        centred = values.astype(jnp.float32) - mean
        squares = jnp.sum((centred * centred).reshape(PATCH // 8, 8, PATCH), axis=0)
        squares = jnp.sum(jnp.sum(squares, axis=0, keepdims=True), axis=1, keepdims=True)
        scale = lax.rsqrt(squares * (1.0 / (PATCH * PATCH)) + 1e-05)
        top = rows[:8] - jnp.where(head8, mean * float(PATCH), zero8)
        return jnp.concatenate([top, rows[8:]], axis=0).astype(jnp.bfloat16), scale

    def transform(rows, scale, target):
        by_cos = dot(rows, table[0])
        by_sin = dot(rows, table[1])
        real = by_cos[8:HALF] + by_sin[HALF + 8 :]
        imag = by_cos[HALF + 8 :] - by_sin[8:HALF]
        cos_last, sin_last = by_cos[HALF : HALF + 8], by_sin[HALF : HALF + 8]
        real8 = by_cos[:8] + jnp.where(head8, zero8, sin_last)
        imag8 = jnp.where(head8, zero8, cos_last) - by_sin[:8]
        last = jnp.concatenate([jnp.where(head8, cos_last, zero8), jnp.where(head8, -sin_last, zero8)], axis=0)
        whole = jnp.concatenate([real8, real, imag8, imag, last], axis=0)
        target[...] = (whole * scale).astype(jnp.bfloat16)

    def direct(j):
        return remote(send.at[j], spec.at[a], spec_send.at[j], spec_recv.at[a], 2 * chip(j + 1) + k, r)

    def hand(j):
        target = passing.at[j] if j < 3 else spec.at[a]
        received = passing_recv.at[j] if j < 3 else spec_recv.at[a]
        return remote(send.at[3 + j], target, spec_send.at[3 + j], received, peer, r)

    def forward(j):
        to = 2 * chip(-(j + 1)) + k
        return remote(passing.at[j], spec.at[peer], passing_send.at[j], spec_recv.at[peer], to, r)

    for j in range(4):
        wait_halo(j)
        rows, scale = analyse(2 * chip(j + 1) + k, k)
        transform(rows, scale, send.at[j] if j < 3 else spec.at[a])
        if j < 3:
            direct(j).start()
        if j == 0:
            anchor_copy(2).wait_recv()
            anchor_copy(0).wait_recv()
            anchor_share(k).start()

    anchor_share(1 - k).wait_recv()
    wait_halo(4)
    ahead = analyse(2 * chip(1) + 1 - k, 1 - k)
    for j in range(4):
        now = ahead
        if j < 3:
            ahead = analyse(2 * chip(j + 2) + 1 - k, 1 - k)
        transform(*now, send.at[3 + j])
        hand(j).start()
        if j > 0:
            hand(j - 1).wait_recv()
            forward(j - 1).start()

    def cross(s, t):
        def part(section, start, stop):
            return spec[section, start:stop, :].astype(jnp.float32)

        def products(a_re, a_im, b_re, b_im):
            return a_re * b_re + a_im * b_im, a_re * b_im - a_im * b_re

        real, imag = products(part(s, 0, HALF), part(s, HALF, PATCH), part(t, 0, HALF), part(t, HALF, PATCH))
        e, f = part(s, PATCH, PATCH + EXTRA), part(t, PATCH, PATCH + EXTRA)
        last_re, last_im = products(e[:8], e[8:], f[:8], f[8:])
        return jnp.concatenate([real[:8] - last_im, real[8:], imag[:8] + last_re, imag[8:]], axis=0).astype(jnp.bfloat16)

    scale = BETA / math.log(2.0) / float(PATCH) ** 4
    group = lax.broadcasted_iota(jnp.int32, (PATCH // 8, 8, PATCH), 0).astype(jnp.float32) * 8.0
    signed_group = jnp.where(group < HALF, group, group - PATCH)

    def correlate(numbers):
        crosses = [cross(n // 2, n // 2 + 1 + n % 2) for n in numbers]
        by_cos = [dot(pair, table[0]) for pair in crosses]
        by_sin = [dot(pair, table[1]) for pair in crosses]
        halves = []
        for c, s in zip(by_cos, by_sin):
            half = jnp.concatenate([c[:HALF] - s[HALF:], s[:HALF] + c[HALF:]], axis=0)
            halves.append(half.astype(jnp.bfloat16))
        full = [dot(table[3], half) for half in halves]
        for n, corr in zip(numbers, full):
            weight = jnp.exp2(corr * scale).reshape(PATCH // 8, 8, PATCH)
            slot = n // 2 + SECTIONS * (n % 2)
            stat_plain[slot] = jnp.sum(weight, axis=0)
            stat_row[slot] = jnp.sum(weight * signed_group, axis=0)

    waits, work = plan()
    for q in range(SECTIONS):
        if q > 0:
            s = pick(waits[q], a)
            remote(send.at[0], spec.at[s], spec_send.at[0], spec_recv.at[s], peer, r).wait_recv()
        for i in range(0, len(work[q]), BATCH):
            correlate([pick(entry, a) for entry in work[q][i : i + BATCH]])

    plain = stat_plain[...]
    sub = lax.broadcasted_iota(jnp.int32, plain.shape, 1).astype(jnp.float32)
    by_row = jnp.sum(stat_row[...] + sub * plain, axis=1)
    plain = jnp.sum(plain, axis=1)
    column = lax.broadcasted_iota(jnp.int32, plain.shape, 1).astype(jnp.float32)
    signed = jnp.where(column < HALF, column, column - PATCH)
    total = jnp.sum(plain, axis=1, keepdims=True)
    shift_row = jnp.sum(by_row, axis=1, keepdims=True) / total / SHIFT_UNIT
    shift_col = jnp.sum(plain * signed, axis=1, keepdims=True) / total / SHIFT_UNIT
    lane = lax.broadcasted_iota(jnp.int32, (SECTIONS, LANES), 1)
    section = lax.broadcasted_iota(jnp.int32, (SECTIONS, LANES), 0)
    lanes = lax.broadcasted_iota(jnp.int32, (1, LANES), 1)
    for lag in (1, 2):
        keep = jnp.zeros((1, LANES), jnp.float32)
        for s in range(SECTIONS - lag):
            both = (1 - missing[s]) * (1 - missing[s + lag]) * valid[0, 0]
            keep = jnp.where(lanes == s, both.astype(jnp.float32), keep)
        for axis, shift in enumerate((shift_row, shift_col)):
            part = shift[(lag - 1) * SECTIONS : lag * SECTIONS]
            line = jnp.sum(jnp.where(lane == section, part, 0.0), axis=0, keepdims=True) * keep
            out_ref[axis, lag - 1] = line.reshape(1, 1, LANES)[:, :, :SECTIONS]

    for m in range(CHIPS + 1):
        each_halo(True, lambda side: halo_copy(m, side).wait_send())
    for j in range(3):
        anchor_copy(j).wait_send()
        direct(j).wait_send()
        forward(j).wait_send()
    anchor_share(k).wait_send()
    for j in range(4):
        hand(j).wait_send()


def body(row_count, sections_img, missing, patch_anchor, block_valid):
    wide = SECTIONS * PATCH
    bf16, f32, i32 = jnp.bfloat16, jnp.float32, jnp.int32
    dma = pltpu.SemaphoreType.DMA
    flow = pl.pallas_call(
        functools.partial(kernel, row_count),
        out_shape=jax.ShapeDtypeStruct((2, 2, 1, 1, SECTIONS), f32),
        in_specs=[pl.BlockSpec(memory_space=pltpu.HBM)] * 5,
        out_specs=pl.BlockSpec(memory_space=pltpu.VMEM),
        scratch_shapes=[
            pltpu.SMEM((1, 1, 2), i32),
            pltpu.SMEM((SECTIONS,), i32),
            pltpu.SMEM((1, 1), i32),
            pltpu.VMEM((PATCH, wide + 2 * LANES), bf16),
            pltpu.VMEM((MARGIN, wide + 2 * LANES), bf16),
            pltpu.VMEM((MARGIN, wide + 2 * LANES), bf16),
            pltpu.VMEM((4, PATCH, PATCH), bf16),
            pltpu.VMEM((2, CHIPS, 8, LANES), f32),
            pltpu.VMEM((7, PATCH + EXTRA, PATCH), bf16),
            pltpu.VMEM((3, PATCH + EXTRA, PATCH), bf16),
            pltpu.VMEM((SECTIONS, PATCH + EXTRA, PATCH), bf16),
            pltpu.VMEM((2 * SECTIONS, 8, PATCH), f32),
            pltpu.VMEM((2 * SECTIONS, 8, PATCH), f32),
            dma((5,)),
            dma((2, CHIPS + 1)),
            dma((2, CHIPS + 1)),
            dma((CHIPS,)),
            dma((CHIPS,)),
            dma((7,)),
            dma((SECTIONS,)),
            dma((3,)),
            dma((3,)),
        ],
        compiler_params=pltpu.CompilerParams(
            collective_id=0, has_side_effects=True, vmem_limit_bytes=55000 * 1024
        ),
        name="flow",
    )(sections_img, jnp.transpose(patch_anchor, (1, 2, 0)), missing, block_valid, jnp.asarray(tables()))
    return jnp.transpose(flow, (0, 1, 4, 2, 3))


def solution(mesh):
    placed = (P("sec", "xy", None), P(), P(None, "xy", "sec"), P("xy", "sec"))
    return jax.shard_map(
        functools.partial(body, mesh.shape["xy"]),
        mesh=mesh,
        in_specs=placed,
        out_specs=P(None, None, None, "xy", "sec"),
        check_vma=False,
    )
```

```python
import functools
import math

import jax
import jax.numpy as jnp
import numpy as np
from jax import lax
from jax.experimental import pallas as pl
from jax.experimental.pallas import tpu as pltpu
from jax.sharding import PartitionSpec as P

PATCH = 256
HALF = PATCH // 2
MARGIN = 64
LANES = 128
SECTIONS = 8
CHIPS = 4
BATCH = 4
BETA = 30.0
SHIFT_UNIT = 8.0
MESH = pl.DeviceIdType.MESH


def tables():
    index = np.arange(PATCH)
    phase = (index[:, None] * index[None, :] % PATCH).astype(np.float32) * np.float32(2.0 * math.pi / PATCH)
    cosine, sine = np.cos(phase), np.sin(phase)
    alternating = np.where(index % 2 == 0, 1.0, -1.0).astype(np.float32)
    analysis = np.concatenate([cosine[:HALF], -sine[:HALF]], axis=0)
    analysis[HALF] = alternating
    synthesis = np.concatenate([2.0 * cosine[:, :HALF], -2.0 * sine[:, :HALF]], axis=1)
    synthesis[:, 0] = 1.0
    synthesis[:, HALF] = alternating
    return np.stack([cosine, sine, analysis, synthesis]).astype(jnp.bfloat16)


def dot(left, right):
    return jnp.dot(left, right, preferred_element_type=jnp.float32)


def plan():
    orders = []
    for a in range(SECTIONS):
        y, k = a // 2, a % 2
        sign = 1 - 2 * k
        same = [2 * ((y - sign * j) % CHIPS) + k for j in range(CHIPS)]
        peer = [2 * ((y + sign * j) % CHIPS) + 1 - k for j in range(CHIPS)]
        orders.append(same + [peer[1], peer[0], peer[2], peer[3]])
    pairs = range(2 * SECTIONS - 3)
    ready = []
    for order in orders:
        rank = {s: i for i, s in enumerate(order)}
        ready.append(sorted((max(rank[n // 2], rank[n // 2 + 1 + n % 2]), n) for n in pairs))
    steps = [max(entry[i][0] for entry in ready) for i in range(len(pairs))]
    waits = [tuple(order[i] for order in orders) for i in range(SECTIONS)]
    work = [[tuple(entry[i][1] for entry in ready) for i in range(len(pairs)) if steps[i] == q] for q in range(SECTIONS)]
    return waits, work


def pick(values, a):
    if max(values) < 8:
        power = (1 + 7 * (a % 2)) * (1 + 63 * (a // 2 % 2)) * (1 + 4095 * (a // 4))
        return sum(v * 8**i for i, v in enumerate(values)) // power % 8
    return 8 * pick([v // 8 for v in values], a) + pick([v % 8 for v in values], a)


def kernel(
    row_count,
    x_ref,
    anchor_ref,
    missing_ref,
    valid_ref,
    table_ref,
    out_ref,
    anchor,
    missing,
    valid,
    own,
    above,
    below,
    table,
    anchors,
    send,
    passing,
    spec,
    stat_plain,
    stat_row,
    local_sem,
    halo_send,
    halo_recv,
    anchor_send,
    anchor_recv,
    spec_send,
    spec_recv,
    passing_recv,
    passing_send,
):
    a = lax.axis_index("sec")
    r = lax.axis_index("xy")
    y, k = a // 2, a % 2
    sign = 1 - 2 * k
    peer = a + sign
    has_next = 1 - (r + 1) // row_count
    has_before = (r + row_count - 1) // row_count
    wide = SECTIONS * PATCH

    def chip(j):
        return (y + sign * j + 2 * CHIPS) % CHIPS

    def local(source, target, i):
        return pltpu.make_async_copy(source, target, local_sem.at[i])

    def remote(source, target, sent, received, to_a, to_r):
        return pltpu.make_async_remote_copy(
            src_ref=source,
            dst_ref=target,
            send_sem=sent,
            recv_sem=received,
            device_id=(to_a, to_r),
            device_id_type=MESH,
        )

    local_own = local(x_ref.at[0], own.at[:, pl.ds(LANES, wide)], 0)
    local_table = local(table_ref, table, 1)
    small = [local(anchor_ref, anchor, 2), local(missing_ref, missing, 3), local(valid_ref, valid, 4)]
    for copy in small:
        copy.start()
    local_own.start()
    local_table.start()

    barrier = pltpu.get_barrier_semaphore()

    @pl.when(has_next == 1)
    def _():
        pl.semaphore_signal(barrier, inc=1, device_id=(a, r + 1), device_id_type=MESH)

    @pl.when(has_before == 1)
    def _():
        pl.semaphore_signal(barrier, inc=1, device_id=(a, r - 1), device_id_type=MESH)

    for j in (1, -1):
        pl.semaphore_signal(barrier, inc=1, device_id=(2 * chip(j) + k, r), device_id_type=MESH)
    pl.semaphore_signal(barrier, inc=1, device_id=(peer, r), device_id_type=MESH)

    @pl.when(has_next == 0)
    def _():
        below[...] = jnp.zeros_like(below)

    @pl.when(has_before == 0)
    def _():
        above[...] = jnp.zeros_like(above)

    own[:, 0:LANES] = jnp.zeros((PATCH, LANES), jnp.bfloat16)
    own[:, LANES + wide :] = jnp.zeros((PATCH, LANES), jnp.bfloat16)
    stat_plain[...] = jnp.ones_like(stat_plain)
    stat_row[...] = jnp.zeros_like(stat_row)
    for copy in small:
        copy.wait()
    me_row = jnp.full((1, LANES), anchor[0, 0, 0], jnp.float32)
    me_col = jnp.full((1, LANES), anchor[0, 0, 1], jnp.float32)
    anchors[k, y] = jnp.concatenate([me_row, me_col, jnp.zeros((6, LANES), jnp.float32)], axis=0)

    local_own.wait()
    pl.semaphore_wait(barrier, 3 + has_next + has_before)

    def anchor_copy(i):
        moved, to = ((y, 1), (y, -1), (chip(1), -1))[i]
        group = anchors.at[k, moved]
        return remote(group, group, anchor_send.at[i], anchor_recv.at[i], 2 * chip(to) + k, r)

    def anchor_share(parity):
        group = anchors.at[parity]
        return remote(group, group, anchor_send.at[3], anchor_recv.at[3], peer, r)

    def halo_copy(m, side):
        if m < CHIPS:
            columns = pl.ds(pl.multiple_of((2 * chip(m + 1) + k) * PATCH, PATCH), 2 * PATCH)
        else:
            columns = pl.ds(pl.multiple_of((1 - k) * wide, PATCH), PATCH)
        rows, ref, to = ((PATCH - MARGIN, above, r + 1), (0, below, r - 1))[side]
        return remote(
            own.at[pl.ds(rows, MARGIN), columns],
            ref.at[:, columns],
            halo_send.at[side, m],
            halo_recv.at[side, m],
            a,
            to,
        )

    def each_halo(sending, act):
        for side in (0, 1):
            there = has_next if (side == 0) == sending else has_before

            @pl.when(there == 1)
            def _():
                act(side)

    anchor_copy(1).start()
    anchor_copy(0).start()

    def start_halo(m):
        each_halo(True, lambda side: halo_copy(m, side).start())

    def wait_halo(m):
        each_halo(False, lambda side: halo_copy(m, side).wait_recv())

    for m in range(CHIPS + 1):
        start_halo(m)

    anchor_copy(1).wait_recv()
    anchor_copy(2).start()
    local_table.wait()

    def cut(c, parity):
        base = pl.multiple_of(c * PATCH + LANES, LANES)
        shift_row = anchors[parity, c // 2, 0:1, :]
        shift_col = anchors[parity, c // 2, 1:2, :]
        sub = lax.broadcasted_iota(jnp.int32, (MARGIN, LANES), 0).astype(jnp.float32)
        lane = lax.broadcasted_iota(jnp.int32, (16, LANES), 1).astype(jnp.float32)

        def mask(condition):
            one = jnp.where(condition, 1.0, 0.0)
            return one.astype(jnp.bfloat16), (1.0 - one).astype(jnp.bfloat16)

        from_below, not_below = mask(sub < shift_row)
        from_above, not_above = mask(sub >= shift_row + MARGIN)
        from_right, not_right = mask(lane < shift_col)
        from_left, not_left = mask(lane >= shift_col + LANES)

        def rows_of(offset):
            lanes = pl.ds(pl.multiple_of(base + offset, LANES), LANES)
            top = below[:, lanes] * from_below + own[0:MARGIN, lanes] * not_below
            middle = own[MARGIN : PATCH - MARGIN, lanes]
            bottom = above[:, lanes] * from_above + own[PATCH - MARGIN :, lanes] * not_above
            return jnp.concatenate([top, middle, bottom], axis=0).reshape(PATCH // 16, 16, LANES)

        left = rows_of(PATCH) * from_right[None] + rows_of(0) * not_right[None]
        right = rows_of(-LANES) * from_left[None] + rows_of(LANES) * not_left[None]
        return jnp.concatenate([left.reshape(PATCH, LANES), right.reshape(PATCH, LANES)], axis=1)

    head8 = lax.broadcasted_iota(jnp.int32, (8, PATCH), 0) == 0
    zero8 = jnp.zeros((8, PATCH), jnp.float32)
    lane8 = lax.broadcasted_iota(jnp.int32, (8, HALF), 1)
    mirror8 = (HALF - lane8) % HALF

    def analyse(c, parity):
        values = cut(c, parity)
        rows = dot(table[2], values)
        mean = jnp.sum(rows[0:1, :], axis=1, keepdims=True) * (1.0 / (PATCH * PATCH))
        centred = values.astype(jnp.float32) - mean
        squares = jnp.sum((centred * centred).reshape(PATCH // 8, 8, PATCH), axis=0)
        squares = jnp.sum(jnp.sum(squares, axis=0, keepdims=True), axis=1, keepdims=True)
        scale = lax.rsqrt(squares * (1.0 / (PATCH * PATCH)) + 1e-05)
        top = rows[:8] - jnp.where(head8, mean * float(PATCH), zero8)
        return jnp.concatenate([top, rows[8:]], axis=0).astype(jnp.bfloat16), scale

    def transform(rows, scale, target):
        by_cos = dot(rows, table[0])
        by_sin = dot(rows, table[1])
        real = by_cos[8:HALF] + by_sin[HALF + 8 :]
        imag = by_cos[HALF + 8 :] - by_sin[8:HALF]
        def mirrored(row):
            re, im = by_cos[row : row + 8], -by_sin[row : row + 8]
            return re[:, :HALF], jnp.where(lane8 == 0, re[:, HALF:], im[:, :HALF])

        zero_re, zero_im = mirrored(0)
        last_re, last_im = mirrored(HALF)
        real8 = jnp.where(head8, jnp.concatenate([zero_re, last_re], axis=1), by_cos[:8] + by_sin[HALF : HALF + 8])
        imag8 = jnp.where(head8, jnp.concatenate([zero_im, last_im], axis=1), by_cos[HALF : HALF + 8] - by_sin[:8])
        whole = jnp.concatenate([real8, real, imag8, imag], axis=0)
        target[...] = (whole * scale).astype(jnp.bfloat16)

    def direct(j):
        return remote(send.at[j], spec.at[a], spec_send.at[j], spec_recv.at[a], 2 * chip(j + 1) + k, r)

    def hand(j):
        target = passing.at[j] if j < 3 else spec.at[a]
        received = passing_recv.at[j] if j < 3 else spec_recv.at[a]
        return remote(send.at[3 + j], target, spec_send.at[3 + j], received, peer, r)

    def forward(j):
        to = 2 * chip(-(j + 1)) + k
        return remote(passing.at[j], spec.at[peer], passing_send.at[j], spec_recv.at[peer], to, r)

    for j in range(4):
        wait_halo(j)
        rows, scale = analyse(2 * chip(j + 1) + k, k)
        transform(rows, scale, send.at[j] if j < 3 else spec.at[a])
        if j < 3:
            direct(j).start()
        if j == 0:
            anchor_copy(2).wait_recv()
            anchor_copy(0).wait_recv()
            anchor_share(k).start()

    anchor_share(1 - k).wait_recv()
    wait_halo(4)
    ahead = analyse(2 * chip(1) + 1 - k, 1 - k)
    for j in range(4):
        now = ahead
        if j < 3:
            ahead = analyse(2 * chip(j + 2) + 1 - k, 1 - k)
        transform(*now, send.at[3 + j])
        hand(j).start()
        if j > 0:
            hand(j - 1).wait_recv()
            forward(j - 1).start()

    def cross(s, t):
        def part(section, start, stop):
            return spec[section, start:stop, :].astype(jnp.float32)

        def products(a_re, a_im, b_re, b_im):
            return a_re * b_re + a_im * b_im, a_re * b_im - a_im * b_re

        a_re, a_im = part(s, 0, HALF), part(s, HALF, PATCH)
        b_re, b_im = part(t, 0, HALF), part(t, HALF, PATCH)
        real, imag = products(a_re, a_im, b_re, b_im)

        def mirrored(side):
            re, im = real[:8, side], imag[:8, side]
            first_one = a_re[:8, side] * b_re[:8, side]
            middle = a_im[:8, side] * b_im[:8, side]
            return jnp.where(lane8 == 0, first_one, re), jnp.where(lane8 == 0, 0.0, im), middle

        zero_re, zero_im, zero_mid = mirrored(slice(0, HALF))
        last_re, last_im, last_mid = mirrored(slice(HALF, PATCH))
        far_re = jnp.where(lane8 == 0, zero_mid, jnp.take_along_axis(zero_re + last_im, mirror8, axis=1))
        far_im = jnp.where(lane8 == 0, last_mid, jnp.take_along_axis(last_re - zero_im, mirror8, axis=1))
        real8 = jnp.concatenate([zero_re - last_im, far_re], axis=1)
        imag8 = jnp.concatenate([zero_im + last_re, far_im], axis=1)
        real8 = jnp.where(head8, real8, real[:8])
        imag8 = jnp.where(head8, imag8, imag[:8])
        return jnp.concatenate([real8, real[8:], imag8, imag[8:]], axis=0).astype(jnp.bfloat16)

    scale = BETA / math.log(2.0) / float(PATCH) ** 4
    group = lax.broadcasted_iota(jnp.int32, (PATCH // 8, 8, PATCH), 0).astype(jnp.float32) * 8.0
    signed_group = jnp.where(group < HALF, group, group - PATCH)

    def correlate(numbers):
        crosses = [cross(n // 2, n // 2 + 1 + n % 2) for n in numbers]
        by_cos = [dot(pair, table[0]) for pair in crosses]
        by_sin = [dot(pair, table[1]) for pair in crosses]
        halves = []
        for c, s in zip(by_cos, by_sin):
            half = jnp.concatenate([c[:HALF] - s[HALF:], s[:HALF] + c[HALF:]], axis=0)
            halves.append(half.astype(jnp.bfloat16))
        full = [dot(table[3], half) for half in halves]
        for n, corr in zip(numbers, full):
            weight = jnp.exp2(corr * scale).reshape(PATCH // 8, 8, PATCH)
            slot = n // 2 + SECTIONS * (n % 2)
            stat_plain[slot] = jnp.sum(weight, axis=0)
            stat_row[slot] = jnp.sum(weight * signed_group, axis=0)

    waits, work = plan()
    for q in range(SECTIONS):
        if q > 0:
            s = pick(waits[q], a)
            remote(send.at[0], spec.at[s], spec_send.at[0], spec_recv.at[s], peer, r).wait_recv()
        for i in range(0, len(work[q]), BATCH):
            correlate([pick(entry, a) for entry in work[q][i : i + BATCH]])

    plain = stat_plain[...]
    sub = lax.broadcasted_iota(jnp.int32, plain.shape, 1).astype(jnp.float32)
    by_row = jnp.sum(stat_row[...] + sub * plain, axis=1)
    plain = jnp.sum(plain, axis=1)
    column = lax.broadcasted_iota(jnp.int32, plain.shape, 1).astype(jnp.float32)
    signed = jnp.where(column < HALF, column, column - PATCH)
    total = jnp.sum(plain, axis=1, keepdims=True)
    shift_row = jnp.sum(by_row, axis=1, keepdims=True) / total / SHIFT_UNIT
    shift_col = jnp.sum(plain * signed, axis=1, keepdims=True) / total / SHIFT_UNIT
    lane = lax.broadcasted_iota(jnp.int32, (SECTIONS, LANES), 1)
    section = lax.broadcasted_iota(jnp.int32, (SECTIONS, LANES), 0)
    lanes = lax.broadcasted_iota(jnp.int32, (1, LANES), 1)
    for lag in (1, 2):
        keep = jnp.zeros((1, LANES), jnp.float32)
        for s in range(SECTIONS - lag):
            both = (1 - missing[s]) * (1 - missing[s + lag]) * valid[0, 0]
            keep = jnp.where(lanes == s, both.astype(jnp.float32), keep)
        for axis, shift in enumerate((shift_row, shift_col)):
            part = shift[(lag - 1) * SECTIONS : lag * SECTIONS]
            line = jnp.sum(jnp.where(lane == section, part, 0.0), axis=0, keepdims=True) * keep
            out_ref[axis, lag - 1] = line.reshape(1, 1, LANES)[:, :, :SECTIONS]

    for m in range(CHIPS + 1):
        each_halo(True, lambda side: halo_copy(m, side).wait_send())
    for j in range(3):
        anchor_copy(j).wait_send()
        direct(j).wait_send()
        forward(j).wait_send()
    anchor_share(k).wait_send()
    for j in range(4):
        hand(j).wait_send()


def body(row_count, sections_img, missing, patch_anchor, block_valid):
    wide = SECTIONS * PATCH
    bf16, f32, i32 = jnp.bfloat16, jnp.float32, jnp.int32
    dma = pltpu.SemaphoreType.DMA
    flow = pl.pallas_call(
        functools.partial(kernel, row_count),
        out_shape=jax.ShapeDtypeStruct((2, 2, 1, 1, SECTIONS), f32),
        in_specs=[pl.BlockSpec(memory_space=pltpu.HBM)] * 5,
        out_specs=pl.BlockSpec(memory_space=pltpu.VMEM),
        scratch_shapes=[
            pltpu.SMEM((1, 1, 2), i32),
            pltpu.SMEM((SECTIONS,), i32),
            pltpu.SMEM((1, 1), i32),
            pltpu.VMEM((PATCH, wide + 2 * LANES), bf16),
            pltpu.VMEM((MARGIN, wide + 2 * LANES), bf16),
            pltpu.VMEM((MARGIN, wide + 2 * LANES), bf16),
            pltpu.VMEM((4, PATCH, PATCH), bf16),
            pltpu.VMEM((2, CHIPS, 8, LANES), f32),
            pltpu.VMEM((7, PATCH, PATCH), bf16),
            pltpu.VMEM((3, PATCH, PATCH), bf16),
            pltpu.VMEM((SECTIONS, PATCH, PATCH), bf16),
            pltpu.VMEM((2 * SECTIONS, 8, PATCH), f32),
            pltpu.VMEM((2 * SECTIONS, 8, PATCH), f32),
            dma((5,)),
            dma((2, CHIPS + 1)),
            dma((2, CHIPS + 1)),
            dma((CHIPS,)),
            dma((CHIPS,)),
            dma((7,)),
            dma((SECTIONS,)),
            dma((3,)),
            dma((3,)),
        ],
        compiler_params=pltpu.CompilerParams(
            collective_id=0, has_side_effects=True, vmem_limit_bytes=55000 * 1024
        ),
        name="flow",
    )(sections_img, jnp.transpose(patch_anchor, (1, 2, 0)), missing, block_valid, jnp.asarray(tables()))
    return jnp.transpose(flow, (0, 1, 4, 2, 3))


def solution(mesh):
    placed = (P("sec", "xy", None), P(), P(None, "xy", "sec"), P("xy", "sec"))
    return jax.shard_map(
        functools.partial(body, mesh.shape["xy"]),
        mesh=mesh,
        in_specs=placed,
        out_specs=P(None, None, None, "xy", "sec"),
        check_vma=False,
    )
```

```python
import functools
import math

import jax
import jax.numpy as jnp
import numpy as np
from jax import lax
from jax.experimental import pallas as pl
from jax.experimental.pallas import tpu as pltpu
from jax.sharding import PartitionSpec as P

PATCH = 256
HALF = PATCH // 2
MARGIN = 64
LANES = 128
SECTIONS = 8
CHIPS = 4
BATCH = 4
BETA = 30.0
SHIFT_UNIT = 8.0
MESH = pl.DeviceIdType.MESH


def tables():
    index = np.arange(PATCH)
    phase = (index[:, None] * index[None, :] % PATCH).astype(np.float32) * np.float32(2.0 * math.pi / PATCH)
    cosine, sine = np.cos(phase), np.sin(phase)
    alternating = np.where(index % 2 == 0, 1.0, -1.0).astype(np.float32)
    analysis = np.concatenate([cosine[:HALF], -sine[:HALF]], axis=0)
    analysis[HALF] = alternating
    synthesis = np.concatenate([2.0 * cosine[:, :HALF], -2.0 * sine[:, :HALF]], axis=1)
    synthesis[:, 0] = 1.0
    synthesis[:, HALF] = alternating
    return np.stack([cosine, sine, analysis, synthesis]).astype(jnp.bfloat16)


def dot(left, right):
    return jnp.dot(left, right, preferred_element_type=jnp.float32)


def plan():
    orders = []
    for a in range(SECTIONS):
        y, k = a // 2, a % 2
        sign = 1 - 2 * k
        same = [2 * ((y - sign * j) % CHIPS) + k for j in range(CHIPS)]
        peer = [2 * ((y + sign * j) % CHIPS) + 1 - k for j in range(CHIPS)]
        orders.append(same + [peer[1], peer[0], peer[2], peer[3]])
    pairs = range(2 * SECTIONS - 3)
    ready = []
    for order in orders:
        rank = {s: i for i, s in enumerate(order)}
        ready.append(sorted((max(rank[n // 2], rank[n // 2 + 1 + n % 2]), n) for n in pairs))
    steps = [max(entry[i][0] for entry in ready) for i in range(len(pairs))]
    waits = [tuple(order[i] for order in orders) for i in range(SECTIONS)]
    work = [[tuple(entry[i][1] for entry in ready) for i in range(len(pairs)) if steps[i] == q] for q in range(SECTIONS)]
    return waits, work


def pick(values, a):
    if max(values) < 8:
        power = (1 + 7 * (a % 2)) * (1 + 63 * (a // 2 % 2)) * (1 + 4095 * (a // 4))
        return sum(v * 8**i for i, v in enumerate(values)) // power % 8
    return 8 * pick([v // 8 for v in values], a) + pick([v % 8 for v in values], a)


def kernel(
    row_count,
    x_ref,
    anchor_ref,
    missing_ref,
    valid_ref,
    table_ref,
    out_ref,
    anchor,
    missing,
    valid,
    own,
    above,
    below,
    table,
    anchors,
    send,
    passing,
    spec,
    stat_plain,
    stat_row,
    local_sem,
    halo_send,
    halo_recv,
    anchor_send,
    anchor_recv,
    spec_send,
    spec_recv,
    passing_recv,
    passing_send,
):
    a = lax.axis_index("sec")
    r = lax.axis_index("xy")
    y, k = a // 2, a % 2
    sign = 1 - 2 * k
    peer = a + sign
    has_next = 1 - (r + 1) // row_count
    has_before = (r + row_count - 1) // row_count
    wide = SECTIONS * PATCH

    def chip(j):
        return (y + sign * j + 2 * CHIPS) % CHIPS

    def local(source, target, i):
        return pltpu.make_async_copy(source, target, local_sem.at[i])

    def remote(source, target, sent, received, to_a, to_r):
        return pltpu.make_async_remote_copy(
            src_ref=source,
            dst_ref=target,
            send_sem=sent,
            recv_sem=received,
            device_id=(to_a, to_r),
            device_id_type=MESH,
        )

    local_own = local(x_ref.at[0], own.at[:, pl.ds(LANES, wide)], 0)
    local_table = local(table_ref, table, 1)
    small = [local(anchor_ref, anchor, 2), local(missing_ref, missing, 3), local(valid_ref, valid, 4)]
    for copy in small:
        copy.start()
    local_own.start()
    local_table.start()

    barrier = pltpu.get_barrier_semaphore()

    @pl.when(has_next == 1)
    def _():
        pl.semaphore_signal(barrier, inc=1, device_id=(a, r + 1), device_id_type=MESH)

    @pl.when(has_before == 1)
    def _():
        pl.semaphore_signal(barrier, inc=1, device_id=(a, r - 1), device_id_type=MESH)

    for j in (1, -1):
        pl.semaphore_signal(barrier, inc=1, device_id=(2 * chip(j) + k, r), device_id_type=MESH)
    pl.semaphore_signal(barrier, inc=1, device_id=(peer, r), device_id_type=MESH)

    @pl.when(has_next == 0)
    def _():
        below[...] = jnp.zeros_like(below)

    @pl.when(has_before == 0)
    def _():
        above[...] = jnp.zeros_like(above)

    own[:, 0:LANES] = jnp.zeros((PATCH, LANES), jnp.bfloat16)
    own[:, LANES + wide :] = jnp.zeros((PATCH, LANES), jnp.bfloat16)
    margin = pl.ds(pl.multiple_of((1 - k) * (wide + LANES), LANES), LANES)
    above[:, margin] = jnp.zeros((MARGIN, LANES), jnp.bfloat16)
    below[:, margin] = jnp.zeros((MARGIN, LANES), jnp.bfloat16)
    stat_plain[...] = jnp.ones_like(stat_plain)
    stat_row[...] = jnp.zeros_like(stat_row)
    for copy in small:
        copy.wait()
    me_row = jnp.full((1, LANES), anchor[0, 0, 0], jnp.float32)
    me_col = jnp.full((1, LANES), anchor[0, 0, 1], jnp.float32)
    anchors[k, y] = jnp.concatenate([me_row, me_col, jnp.zeros((6, LANES), jnp.float32)], axis=0)

    local_own.wait()
    pl.semaphore_wait(barrier, 3 + has_next + has_before)

    def anchor_copy(i):
        moved, to = ((y, 1), (y, -1), (chip(1), -1))[i]
        group = anchors.at[k, moved]
        return remote(group, group, anchor_send.at[i], anchor_recv.at[i], 2 * chip(to) + k, r)

    def anchor_share(parity):
        group = anchors.at[parity]
        return remote(group, group, anchor_send.at[3], anchor_recv.at[3], peer, r)

    def halo_copy(m, side):
        if m < CHIPS:
            columns = pl.ds(pl.multiple_of((2 * chip(m + 1) + k) * PATCH, PATCH), 2 * PATCH)
        else:
            columns = pl.ds(pl.multiple_of((1 - k) * wide + k * LANES, LANES), LANES)
        rows, ref, to = ((PATCH - MARGIN, above, r + 1), (0, below, r - 1))[side]
        return remote(
            own.at[pl.ds(rows, MARGIN), columns],
            ref.at[:, columns],
            halo_send.at[side, m],
            halo_recv.at[side, m],
            a,
            to,
        )

    def each_halo(sending, act):
        for side in (0, 1):
            there = has_next if (side == 0) == sending else has_before

            @pl.when(there == 1)
            def _():
                act(side)

    anchor_copy(1).start()
    anchor_copy(0).start()

    def start_halo(m):
        each_halo(True, lambda side: halo_copy(m, side).start())

    def wait_halo(m):
        each_halo(False, lambda side: halo_copy(m, side).wait_recv())

    for m in range(CHIPS + 1):
        start_halo(m)

    anchor_copy(1).wait_recv()
    anchor_copy(2).start()
    local_table.wait()

    def cut(c, parity):
        base = pl.multiple_of(c * PATCH + LANES, LANES)
        shift_row = anchors[parity, c // 2, 0:1, :]
        shift_col = anchors[parity, c // 2, 1:2, :]
        sub = lax.broadcasted_iota(jnp.int32, (MARGIN, LANES), 0).astype(jnp.float32)
        lane = lax.broadcasted_iota(jnp.int32, (16, LANES), 1).astype(jnp.float32)

        def mask(condition):
            one = jnp.where(condition, 1.0, 0.0)
            return one.astype(jnp.bfloat16), (1.0 - one).astype(jnp.bfloat16)

        from_below, not_below = mask(sub < shift_row)
        from_above, not_above = mask(sub >= shift_row + MARGIN)
        from_right, not_right = mask(lane < shift_col)
        from_left, not_left = mask(lane >= shift_col + LANES)

        def rows_of(offset):
            lanes = pl.ds(pl.multiple_of(base + offset, LANES), LANES)
            top = below[:, lanes] * from_below + own[0:MARGIN, lanes] * not_below
            middle = own[MARGIN : PATCH - MARGIN, lanes]
            bottom = above[:, lanes] * from_above + own[PATCH - MARGIN :, lanes] * not_above
            return jnp.concatenate([top, middle, bottom], axis=0).reshape(PATCH // 16, 16, LANES)

        left = rows_of(PATCH) * from_right[None] + rows_of(0) * not_right[None]
        right = rows_of(-LANES) * from_left[None] + rows_of(LANES) * not_left[None]
        return jnp.concatenate([left.reshape(PATCH, LANES), right.reshape(PATCH, LANES)], axis=1)

    head8 = lax.broadcasted_iota(jnp.int32, (8, PATCH), 0) == 0
    zero8 = jnp.zeros((8, PATCH), jnp.float32)
    lane8 = lax.broadcasted_iota(jnp.int32, (8, HALF), 1)
    mirror8 = (HALF - lane8) % HALF

    def analyse(c, parity):
        values = cut(c, parity)
        rows = dot(table[2], values)
        mean = jnp.sum(rows[0:1, :], axis=1, keepdims=True) * (1.0 / (PATCH * PATCH))
        centred = values.astype(jnp.float32) - mean
        squares = jnp.sum((centred * centred).reshape(PATCH // 8, 8, PATCH), axis=0)
        squares = jnp.sum(jnp.sum(squares, axis=0, keepdims=True), axis=1, keepdims=True)
        scale = lax.rsqrt(squares * (1.0 / (PATCH * PATCH)) + 1e-05)
        top = rows[:8] - jnp.where(head8, mean * float(PATCH), zero8)
        return jnp.concatenate([top, rows[8:]], axis=0).astype(jnp.bfloat16), scale

    def transform(rows, scale, target):
        by_cos = dot(rows, table[0])
        by_sin = dot(rows, table[1])
        real = by_cos[8:HALF] + by_sin[HALF + 8 :]
        imag = by_cos[HALF + 8 :] - by_sin[8:HALF]
        def mirrored(row):
            re, im = by_cos[row : row + 8], -by_sin[row : row + 8]
            return re[:, :HALF], jnp.where(lane8 == 0, re[:, HALF:], im[:, :HALF])

        zero_re, zero_im = mirrored(0)
        last_re, last_im = mirrored(HALF)
        real8 = jnp.where(head8, jnp.concatenate([zero_re, last_re], axis=1), by_cos[:8] + by_sin[HALF : HALF + 8])
        imag8 = jnp.where(head8, jnp.concatenate([zero_im, last_im], axis=1), by_cos[HALF : HALF + 8] - by_sin[:8])
        whole = jnp.concatenate([real8, real, imag8, imag], axis=0)
        target[...] = (whole * scale).astype(jnp.bfloat16)

    def direct(j):
        return remote(send.at[j], spec.at[a], spec_send.at[j], spec_recv.at[a], 2 * chip(j + 1) + k, r)

    def hand(j):
        target = passing.at[j] if j < 3 else spec.at[a]
        received = passing_recv.at[j] if j < 3 else spec_recv.at[a]
        return remote(send.at[3 + j], target, spec_send.at[3 + j], received, peer, r)

    def forward(j):
        to = 2 * chip(-(j + 1)) + k
        return remote(passing.at[j], spec.at[peer], passing_send.at[j], spec_recv.at[peer], to, r)

    for j in range(4):
        wait_halo(j)
        rows, scale = analyse(2 * chip(j + 1) + k, k)
        transform(rows, scale, send.at[j] if j < 3 else spec.at[a])
        if j < 3:
            direct(j).start()
        if j == 0:
            anchor_copy(2).wait_recv()
            anchor_copy(0).wait_recv()
            anchor_share(k).start()

    anchor_share(1 - k).wait_recv()
    wait_halo(4)
    ahead = analyse(2 * chip(1) + 1 - k, 1 - k)
    for j in range(4):
        now = ahead
        if j < 3:
            ahead = analyse(2 * chip(j + 2) + 1 - k, 1 - k)
        transform(*now, send.at[3 + j])
        hand(j).start()
        if j > 0:
            hand(j - 1).wait_recv()
            forward(j - 1).start()

    def cross(s, t):
        def part(section, start, stop):
            return spec[section, start:stop, :].astype(jnp.float32)

        def products(a_re, a_im, b_re, b_im):
            return a_re * b_re + a_im * b_im, a_re * b_im - a_im * b_re

        a_re, a_im = part(s, 0, HALF), part(s, HALF, PATCH)
        b_re, b_im = part(t, 0, HALF), part(t, HALF, PATCH)
        real, imag = products(a_re, a_im, b_re, b_im)

        def mirrored(side):
            re, im = real[:8, side], imag[:8, side]
            first_one = a_re[:8, side] * b_re[:8, side]
            middle = a_im[:8, side] * b_im[:8, side]
            return jnp.where(lane8 == 0, first_one, re), jnp.where(lane8 == 0, 0.0, im), middle

        zero_re, zero_im, zero_mid = mirrored(slice(0, HALF))
        last_re, last_im, last_mid = mirrored(slice(HALF, PATCH))
        far_re = jnp.where(lane8 == 0, zero_mid, jnp.take_along_axis(zero_re + last_im, mirror8, axis=1))
        far_im = jnp.where(lane8 == 0, last_mid, jnp.take_along_axis(last_re - zero_im, mirror8, axis=1))
        real8 = jnp.concatenate([zero_re - last_im, far_re], axis=1)
        imag8 = jnp.concatenate([zero_im + last_re, far_im], axis=1)
        real8 = jnp.where(head8, real8, real[:8])
        imag8 = jnp.where(head8, imag8, imag[:8])
        return jnp.concatenate([real8, real[8:], imag8, imag[8:]], axis=0).astype(jnp.bfloat16)

    scale = BETA / math.log(2.0) / float(PATCH) ** 4
    group = lax.broadcasted_iota(jnp.int32, (PATCH // 8, 8, PATCH), 0).astype(jnp.float32) * 8.0
    signed_group = jnp.where(group < HALF, group, group - PATCH)

    def correlate(numbers):
        crosses = [cross(n // 2, n // 2 + 1 + n % 2) for n in numbers]
        by_cos = [dot(pair, table[0]) for pair in crosses]
        by_sin = [dot(pair, table[1]) for pair in crosses]
        halves = []
        for c, s in zip(by_cos, by_sin):
            half = jnp.concatenate([c[:HALF] - s[HALF:], s[:HALF] + c[HALF:]], axis=0)
            halves.append(half.astype(jnp.bfloat16))
        full = [dot(table[3], half) for half in halves]
        for n, corr in zip(numbers, full):
            weight = jnp.exp2(corr * scale).reshape(PATCH // 8, 8, PATCH)
            slot = n // 2 + SECTIONS * (n % 2)
            stat_plain[slot] = jnp.sum(weight, axis=0)
            stat_row[slot] = jnp.sum(weight * signed_group, axis=0)

    waits, work = plan()
    for q in range(SECTIONS):
        if q > 0:
            s = pick(waits[q], a)
            remote(send.at[0], spec.at[s], spec_send.at[0], spec_recv.at[s], peer, r).wait_recv()
        for i in range(0, len(work[q]), BATCH):
            correlate([pick(entry, a) for entry in work[q][i : i + BATCH]])

    plain = stat_plain[...]
    sub = lax.broadcasted_iota(jnp.int32, plain.shape, 1).astype(jnp.float32)
    by_row = jnp.sum(stat_row[...] + sub * plain, axis=1)
    plain = jnp.sum(plain, axis=1)
    column = lax.broadcasted_iota(jnp.int32, plain.shape, 1).astype(jnp.float32)
    signed = jnp.where(column < HALF, column, column - PATCH)
    total = jnp.sum(plain, axis=1, keepdims=True)
    shift_row = jnp.sum(by_row, axis=1, keepdims=True) / total / SHIFT_UNIT
    shift_col = jnp.sum(plain * signed, axis=1, keepdims=True) / total / SHIFT_UNIT
    lane = lax.broadcasted_iota(jnp.int32, (SECTIONS, LANES), 1)
    section = lax.broadcasted_iota(jnp.int32, (SECTIONS, LANES), 0)
    lanes = lax.broadcasted_iota(jnp.int32, (1, LANES), 1)
    for lag in (1, 2):
        keep = jnp.zeros((1, LANES), jnp.float32)
        for s in range(SECTIONS - lag):
            both = (1 - missing[s]) * (1 - missing[s + lag]) * valid[0, 0]
            keep = jnp.where(lanes == s, both.astype(jnp.float32), keep)
        for axis, shift in enumerate((shift_row, shift_col)):
            part = shift[(lag - 1) * SECTIONS : lag * SECTIONS]
            line = jnp.sum(jnp.where(lane == section, part, 0.0), axis=0, keepdims=True) * keep
            out_ref[axis, lag - 1] = line.reshape(1, 1, LANES)[:, :, :SECTIONS]

    for m in range(CHIPS + 1):
        each_halo(True, lambda side: halo_copy(m, side).wait_send())
    for j in range(3):
        anchor_copy(j).wait_send()
        direct(j).wait_send()
        forward(j).wait_send()
    anchor_share(k).wait_send()
    for j in range(4):
        hand(j).wait_send()


def body(row_count, sections_img, missing, patch_anchor, block_valid):
    wide = SECTIONS * PATCH
    bf16, f32, i32 = jnp.bfloat16, jnp.float32, jnp.int32
    dma = pltpu.SemaphoreType.DMA
    flow = pl.pallas_call(
        functools.partial(kernel, row_count),
        out_shape=jax.ShapeDtypeStruct((2, 2, 1, 1, SECTIONS), f32),
        in_specs=[pl.BlockSpec(memory_space=pltpu.HBM)] * 5,
        out_specs=pl.BlockSpec(memory_space=pltpu.VMEM),
        scratch_shapes=[
            pltpu.SMEM((1, 1, 2), i32),
            pltpu.SMEM((SECTIONS,), i32),
            pltpu.SMEM((1, 1), i32),
            pltpu.VMEM((PATCH, wide + 2 * LANES), bf16),
            pltpu.VMEM((MARGIN, wide + 2 * LANES), bf16),
            pltpu.VMEM((MARGIN, wide + 2 * LANES), bf16),
            pltpu.VMEM((4, PATCH, PATCH), bf16),
            pltpu.VMEM((2, CHIPS, 8, LANES), f32),
            pltpu.VMEM((7, PATCH, PATCH), bf16),
            pltpu.VMEM((3, PATCH, PATCH), bf16),
            pltpu.VMEM((SECTIONS, PATCH, PATCH), bf16),
            pltpu.VMEM((2 * SECTIONS, 8, PATCH), f32),
            pltpu.VMEM((2 * SECTIONS, 8, PATCH), f32),
            dma((5,)),
            dma((2, CHIPS + 1)),
            dma((2, CHIPS + 1)),
            dma((CHIPS,)),
            dma((CHIPS,)),
            dma((7,)),
            dma((SECTIONS,)),
            dma((3,)),
            dma((3,)),
        ],
        compiler_params=pltpu.CompilerParams(
            collective_id=0, has_side_effects=True, vmem_limit_bytes=55000 * 1024
        ),
        name="flow",
    )(sections_img, jnp.transpose(patch_anchor, (1, 2, 0)), missing, block_valid, jnp.asarray(tables()))
    return jnp.transpose(flow, (0, 1, 4, 2, 3))


def solution(mesh):
    placed = (P("sec", "xy", None), P(), P(None, "xy", "sec"), P("xy", "sec"))
    return jax.shard_map(
        functools.partial(body, mesh.shape["xy"]),
        mesh=mesh,
        in_specs=placed,
        out_specs=P(None, None, None, "xy", "sec"),
        check_vma=False,
    )
```

```python
import functools
import math

import jax
import jax.numpy as jnp
import numpy as np
from jax import lax
from jax.experimental import pallas as pl
from jax.experimental.pallas import tpu as pltpu
from jax.sharding import PartitionSpec as P

PATCH = 256
HALF = PATCH // 2
MARGIN = 64
LANES = 128
SECTIONS = 8
CHIPS = 4
BATCH = 13
BETA = 30.0
SHIFT_UNIT = 8.0
MESH = pl.DeviceIdType.MESH


def tables():
    index = np.arange(PATCH)
    phase = (index[:, None] * index[None, :] % PATCH).astype(np.float32) * np.float32(2.0 * math.pi / PATCH)
    cosine, sine = np.cos(phase), np.sin(phase)
    alternating = np.where(index % 2 == 0, 1.0, -1.0).astype(np.float32)
    analysis = np.concatenate([cosine[:HALF], -sine[:HALF]], axis=0)
    analysis[HALF] = alternating
    synthesis = np.concatenate([2.0 * cosine[:, :HALF], -2.0 * sine[:, :HALF]], axis=1)
    synthesis[:, 0] = 1.0
    synthesis[:, HALF] = alternating
    return np.stack([cosine, sine, analysis, synthesis]).astype(jnp.bfloat16)


def dot(left, right):
    return jnp.dot(left, right, preferred_element_type=jnp.float32)


def plan():
    orders = []
    for a in range(SECTIONS):
        y, k = a // 2, a % 2
        sign = 1 - 2 * k
        same = [2 * ((y - sign * j) % CHIPS) + k for j in range(CHIPS)]
        peer = [2 * ((y + sign * j) % CHIPS) + 1 - k for j in range(CHIPS)]
        orders.append(same + [peer[1], peer[0], peer[2], peer[3]])
    pairs = range(2 * SECTIONS - 3)
    ready = []
    for order in orders:
        rank = {s: i for i, s in enumerate(order)}
        ready.append(sorted((max(rank[n // 2], rank[n // 2 + 1 + n % 2]), n) for n in pairs))
    steps = [max(entry[i][0] for entry in ready) for i in range(len(pairs))]
    waits = [tuple(order[i] for order in orders) for i in range(SECTIONS)]
    work = [[tuple(entry[i][1] for entry in ready) for i in range(len(pairs)) if steps[i] == q] for q in range(SECTIONS)]
    return waits, work


def pick(values, a):
    if max(values) < 8:
        power = (1 + 7 * (a % 2)) * (1 + 63 * (a // 2 % 2)) * (1 + 4095 * (a // 4))
        return sum(v * 8**i for i, v in enumerate(values)) // power % 8
    return 8 * pick([v // 8 for v in values], a) + pick([v % 8 for v in values], a)


def kernel(
    row_count,
    x_ref,
    anchor_ref,
    missing_ref,
    valid_ref,
    table_ref,
    out_ref,
    anchor,
    missing,
    valid,
    own,
    above,
    below,
    table,
    anchors,
    send,
    passing,
    spec,
    stat_plain,
    stat_row,
    local_sem,
    halo_send,
    halo_recv,
    anchor_send,
    anchor_recv,
    spec_send,
    spec_recv,
    passing_recv,
    passing_send,
):
    a = lax.axis_index("sec")
    r = lax.axis_index("xy")
    y, k = a // 2, a % 2
    sign = 1 - 2 * k
    peer = a + sign
    has_next = 1 - (r + 1) // row_count
    has_before = (r + row_count - 1) // row_count
    wide = SECTIONS * PATCH

    def chip(j):
        return (y + sign * j + 2 * CHIPS) % CHIPS

    def local(source, target, i):
        return pltpu.make_async_copy(source, target, local_sem.at[i])

    def remote(source, target, sent, received, to_a, to_r):
        return pltpu.make_async_remote_copy(
            src_ref=source,
            dst_ref=target,
            send_sem=sent,
            recv_sem=received,
            device_id=(to_a, to_r),
            device_id_type=MESH,
        )

    local_own = local(x_ref.at[0], own.at[:, pl.ds(LANES, wide)], 0)
    local_table = local(table_ref, table, 1)
    small = [local(anchor_ref, anchor, 2), local(missing_ref, missing, 3), local(valid_ref, valid, 4)]
    for copy in small:
        copy.start()
    local_own.start()
    local_table.start()

    barrier = pltpu.get_barrier_semaphore()

    @pl.when(has_next == 1)
    def _():
        pl.semaphore_signal(barrier, inc=1, device_id=(a, r + 1), device_id_type=MESH)

    @pl.when(has_before == 1)
    def _():
        pl.semaphore_signal(barrier, inc=1, device_id=(a, r - 1), device_id_type=MESH)

    for j in (1, -1):
        pl.semaphore_signal(barrier, inc=1, device_id=(2 * chip(j) + k, r), device_id_type=MESH)
    pl.semaphore_signal(barrier, inc=1, device_id=(peer, r), device_id_type=MESH)

    @pl.when(has_next == 0)
    def _():
        below[...] = jnp.zeros_like(below)

    @pl.when(has_before == 0)
    def _():
        above[...] = jnp.zeros_like(above)

    own[:, 0:LANES] = jnp.zeros((PATCH, LANES), jnp.bfloat16)
    own[:, LANES + wide :] = jnp.zeros((PATCH, LANES), jnp.bfloat16)
    margin = pl.ds(pl.multiple_of((1 - k) * (wide + LANES), LANES), LANES)
    above[:, margin] = jnp.zeros((MARGIN, LANES), jnp.bfloat16)
    below[:, margin] = jnp.zeros((MARGIN, LANES), jnp.bfloat16)
    stat_plain[...] = jnp.ones_like(stat_plain)
    stat_row[...] = jnp.zeros_like(stat_row)
    for copy in small:
        copy.wait()
    me_row = jnp.full((1, LANES), anchor[0, 0, 0], jnp.float32)
    me_col = jnp.full((1, LANES), anchor[0, 0, 1], jnp.float32)
    anchors[k, y] = jnp.concatenate([me_row, me_col, jnp.zeros((6, LANES), jnp.float32)], axis=0)

    local_own.wait()
    pl.semaphore_wait(barrier, 3 + has_next + has_before)

    def anchor_copy(i):
        moved, to = ((y, 1), (y, -1), (chip(1), -1))[i]
        group = anchors.at[k, moved]
        return remote(group, group, anchor_send.at[i], anchor_recv.at[i], 2 * chip(to) + k, r)

    def anchor_share(parity):
        group = anchors.at[parity]
        return remote(group, group, anchor_send.at[3], anchor_recv.at[3], peer, r)

    def halo_copy(m, side):
        if m < CHIPS:
            columns = pl.ds(pl.multiple_of((2 * chip(m + 1) + k) * PATCH, PATCH), 2 * PATCH)
        else:
            columns = pl.ds(pl.multiple_of((1 - k) * wide + k * LANES, LANES), LANES)
        rows, ref, to = ((PATCH - MARGIN, above, r + 1), (0, below, r - 1))[side]
        return remote(
            own.at[pl.ds(rows, MARGIN), columns],
            ref.at[:, columns],
            halo_send.at[side, m],
            halo_recv.at[side, m],
            a,
            to,
        )

    def each_halo(sending, act):
        for side in (0, 1):
            there = has_next if (side == 0) == sending else has_before

            @pl.when(there == 1)
            def _():
                act(side)

    anchor_copy(1).start()
    anchor_copy(0).start()

    def start_halo(m):
        each_halo(True, lambda side: halo_copy(m, side).start())

    def wait_halo(m):
        each_halo(False, lambda side: halo_copy(m, side).wait_recv())

    for m in range(CHIPS + 1):
        start_halo(m)

    anchor_copy(1).wait_recv()
    anchor_copy(2).start()
    local_table.wait()

    def cut(c, parity):
        base = pl.multiple_of(c * PATCH + LANES, LANES)
        shift_row = anchors[parity, c // 2, 0:1, :]
        shift_col = anchors[parity, c // 2, 1:2, :]
        sub = lax.broadcasted_iota(jnp.int32, (MARGIN, LANES), 0).astype(jnp.float32)
        lane = lax.broadcasted_iota(jnp.int32, (16, LANES), 1).astype(jnp.float32)

        def mask(condition):
            one = jnp.where(condition, 1.0, 0.0)
            return one.astype(jnp.bfloat16), (1.0 - one).astype(jnp.bfloat16)

        from_below, not_below = mask(sub < shift_row)
        from_above, not_above = mask(sub >= shift_row + MARGIN)
        from_right, not_right = mask(lane < shift_col)
        from_left, not_left = mask(lane >= shift_col + LANES)

        def rows_of(offset):
            lanes = pl.ds(pl.multiple_of(base + offset, LANES), LANES)
            top = below[:, lanes] * from_below + own[0:MARGIN, lanes] * not_below
            middle = own[MARGIN : PATCH - MARGIN, lanes]
            bottom = above[:, lanes] * from_above + own[PATCH - MARGIN :, lanes] * not_above
            return jnp.concatenate([top, middle, bottom], axis=0).reshape(PATCH // 16, 16, LANES)

        left = rows_of(PATCH) * from_right[None] + rows_of(0) * not_right[None]
        right = rows_of(-LANES) * from_left[None] + rows_of(LANES) * not_left[None]
        return jnp.concatenate([left.reshape(PATCH, LANES), right.reshape(PATCH, LANES)], axis=1)

    head8 = lax.broadcasted_iota(jnp.int32, (8, PATCH), 0) == 0
    zero8 = jnp.zeros((8, PATCH), jnp.float32)
    lane8 = lax.broadcasted_iota(jnp.int32, (8, HALF), 1)
    mirror8 = (HALF - lane8) % HALF

    def analyse(c, parity):
        values = cut(c, parity)
        rows = dot(table[2], values)
        mean = jnp.sum(rows[0:1, :], axis=1, keepdims=True) * (1.0 / (PATCH * PATCH))
        centred = values.astype(jnp.float32) - mean
        squares = jnp.sum((centred * centred).reshape(PATCH // 8, 8, PATCH), axis=0)
        squares = jnp.sum(jnp.sum(squares, axis=0, keepdims=True), axis=1, keepdims=True)
        scale = lax.rsqrt(squares * (1.0 / (PATCH * PATCH)) + 1e-05)
        top = rows[:8] - jnp.where(head8, mean * float(PATCH), zero8)
        return jnp.concatenate([top, rows[8:]], axis=0).astype(jnp.bfloat16), scale

    def transform(rows, scale, target):
        by_cos = dot(rows, table[0])
        by_sin = dot(rows, table[1])
        real = by_cos[8:HALF] + by_sin[HALF + 8 :]
        imag = by_cos[HALF + 8 :] - by_sin[8:HALF]
        def mirrored(row):
            re, im = by_cos[row : row + 8], -by_sin[row : row + 8]
            return re[:, :HALF], jnp.where(lane8 == 0, re[:, HALF:], im[:, :HALF])

        zero_re, zero_im = mirrored(0)
        last_re, last_im = mirrored(HALF)
        real8 = jnp.where(head8, jnp.concatenate([zero_re, last_re], axis=1), by_cos[:8] + by_sin[HALF : HALF + 8])
        imag8 = jnp.where(head8, jnp.concatenate([zero_im, last_im], axis=1), by_cos[HALF : HALF + 8] - by_sin[:8])
        whole = jnp.concatenate([real8, real, imag8, imag], axis=0)
        target[...] = (whole * scale).astype(jnp.bfloat16)

    def direct(j):
        return remote(send.at[j], spec.at[a], spec_send.at[j], spec_recv.at[a], 2 * chip(j + 1) + k, r)

    def hand(j):
        target = passing.at[j] if j < 3 else spec.at[a]
        received = passing_recv.at[j] if j < 3 else spec_recv.at[a]
        return remote(send.at[3 + j], target, spec_send.at[3 + j], received, peer, r)

    def forward(j):
        to = 2 * chip(-(j + 1)) + k
        return remote(passing.at[j], spec.at[peer], passing_send.at[j], spec_recv.at[peer], to, r)

    for j in range(4):
        wait_halo(j)
        rows, scale = analyse(2 * chip(j + 1) + k, k)
        transform(rows, scale, send.at[j] if j < 3 else spec.at[a])
        if j < 3:
            direct(j).start()
        if j == 0:
            anchor_copy(2).wait_recv()
            anchor_copy(0).wait_recv()
            anchor_share(k).start()

    anchor_share(1 - k).wait_recv()
    wait_halo(4)
    ahead = analyse(2 * chip(1) + 1 - k, 1 - k)
    for j in range(4):
        now = ahead
        if j < 3:
            ahead = analyse(2 * chip(j + 2) + 1 - k, 1 - k)
        transform(*now, send.at[3 + j])
        hand(j).start()
        if j > 0:
            hand(j - 1).wait_recv()
            forward(j - 1).start()

    def cross(s, t):
        def part(section, start, stop):
            return spec[section, start:stop, :].astype(jnp.float32)

        def products(a_re, a_im, b_re, b_im):
            return a_re * b_re + a_im * b_im, a_re * b_im - a_im * b_re

        a_re, a_im = part(s, 0, HALF), part(s, HALF, PATCH)
        b_re, b_im = part(t, 0, HALF), part(t, HALF, PATCH)
        real, imag = products(a_re, a_im, b_re, b_im)

        def mirrored(side):
            re, im = real[:8, side], imag[:8, side]
            first_one = a_re[:8, side] * b_re[:8, side]
            middle = a_im[:8, side] * b_im[:8, side]
            return jnp.where(lane8 == 0, first_one, re), jnp.where(lane8 == 0, 0.0, im), middle

        zero_re, zero_im, zero_mid = mirrored(slice(0, HALF))
        last_re, last_im, last_mid = mirrored(slice(HALF, PATCH))
        far_re = jnp.where(lane8 == 0, zero_mid, jnp.take_along_axis(zero_re + last_im, mirror8, axis=1))
        far_im = jnp.where(lane8 == 0, last_mid, jnp.take_along_axis(last_re - zero_im, mirror8, axis=1))
        real8 = jnp.concatenate([zero_re - last_im, far_re], axis=1)
        imag8 = jnp.concatenate([zero_im + last_re, far_im], axis=1)
        real8 = jnp.where(head8, real8, real[:8])
        imag8 = jnp.where(head8, imag8, imag[:8])
        return jnp.concatenate([real8, real[8:], imag8, imag[8:]], axis=0).astype(jnp.bfloat16)

    scale = BETA / math.log(2.0) / float(PATCH) ** 4
    group = lax.broadcasted_iota(jnp.int32, (PATCH // 8, 8, PATCH), 0).astype(jnp.float32) * 8.0
    signed_group = jnp.where(group < HALF, group, group - PATCH)

    def correlate(numbers):
        crosses = [cross(n // 2, n // 2 + 1 + n % 2) for n in numbers]
        by_cos = [dot(pair, table[0]) for pair in crosses]
        by_sin = [dot(pair, table[1]) for pair in crosses]
        halves = []
        for c, s in zip(by_cos, by_sin):
            half = jnp.concatenate([c[:HALF] - s[HALF:], s[:HALF] + c[HALF:]], axis=0)
            halves.append(half.astype(jnp.bfloat16))
        full = [dot(table[3], half) for half in halves]
        for n, corr in zip(numbers, full):
            weight = jnp.exp2(corr * scale).reshape(PATCH // 8, 8, PATCH)
            slot = n // 2 + SECTIONS * (n % 2)
            stat_plain[slot] = jnp.sum(weight, axis=0)
            stat_row[slot] = jnp.sum(weight * signed_group, axis=0)

    waits, work = plan()
    for q in range(SECTIONS):
        if q > 0:
            s = pick(waits[q], a)
            remote(send.at[0], spec.at[s], spec_send.at[0], spec_recv.at[s], peer, r).wait_recv()
        for i in range(0, len(work[q]), BATCH):
            correlate([pick(entry, a) for entry in work[q][i : i + BATCH]])

    plain = stat_plain[...]
    sub = lax.broadcasted_iota(jnp.int32, plain.shape, 1).astype(jnp.float32)
    by_row = jnp.sum(stat_row[...] + sub * plain, axis=1)
    plain = jnp.sum(plain, axis=1)
    column = lax.broadcasted_iota(jnp.int32, plain.shape, 1).astype(jnp.float32)
    signed = jnp.where(column < HALF, column, column - PATCH)
    total = jnp.sum(plain, axis=1, keepdims=True)
    shift_row = jnp.sum(by_row, axis=1, keepdims=True) / total / SHIFT_UNIT
    shift_col = jnp.sum(plain * signed, axis=1, keepdims=True) / total / SHIFT_UNIT
    lane = lax.broadcasted_iota(jnp.int32, (SECTIONS, LANES), 1)
    section = lax.broadcasted_iota(jnp.int32, (SECTIONS, LANES), 0)
    lanes = lax.broadcasted_iota(jnp.int32, (1, LANES), 1)
    for lag in (1, 2):
        keep = jnp.zeros((1, LANES), jnp.float32)
        for s in range(SECTIONS - lag):
            both = (1 - missing[s]) * (1 - missing[s + lag]) * valid[0, 0]
            keep = jnp.where(lanes == s, both.astype(jnp.float32), keep)
        for axis, shift in enumerate((shift_row, shift_col)):
            part = shift[(lag - 1) * SECTIONS : lag * SECTIONS]
            line = jnp.sum(jnp.where(lane == section, part, 0.0), axis=0, keepdims=True) * keep
            out_ref[axis, lag - 1] = line.reshape(1, 1, LANES)[:, :, :SECTIONS]

    for m in range(CHIPS + 1):
        each_halo(True, lambda side: halo_copy(m, side).wait_send())
    for j in range(3):
        anchor_copy(j).wait_send()
        direct(j).wait_send()
        forward(j).wait_send()
    anchor_share(k).wait_send()
    for j in range(4):
        hand(j).wait_send()


def body(row_count, sections_img, missing, patch_anchor, block_valid):
    wide = SECTIONS * PATCH
    bf16, f32, i32 = jnp.bfloat16, jnp.float32, jnp.int32
    dma = pltpu.SemaphoreType.DMA
    flow = pl.pallas_call(
        functools.partial(kernel, row_count),
        out_shape=jax.ShapeDtypeStruct((2, 2, 1, 1, SECTIONS), f32),
        in_specs=[pl.BlockSpec(memory_space=pltpu.HBM)] * 5,
        out_specs=pl.BlockSpec(memory_space=pltpu.VMEM),
        scratch_shapes=[
            pltpu.SMEM((1, 1, 2), i32),
            pltpu.SMEM((SECTIONS,), i32),
            pltpu.SMEM((1, 1), i32),
            pltpu.VMEM((PATCH, wide + 2 * LANES), bf16),
            pltpu.VMEM((MARGIN, wide + 2 * LANES), bf16),
            pltpu.VMEM((MARGIN, wide + 2 * LANES), bf16),
            pltpu.VMEM((4, PATCH, PATCH), bf16),
            pltpu.VMEM((2, CHIPS, 8, LANES), f32),
            pltpu.VMEM((7, PATCH, PATCH), bf16),
            pltpu.VMEM((3, PATCH, PATCH), bf16),
            pltpu.VMEM((SECTIONS, PATCH, PATCH), bf16),
            pltpu.VMEM((2 * SECTIONS, 8, PATCH), f32),
            pltpu.VMEM((2 * SECTIONS, 8, PATCH), f32),
            dma((5,)),
            dma((2, CHIPS + 1)),
            dma((2, CHIPS + 1)),
            dma((CHIPS,)),
            dma((CHIPS,)),
            dma((7,)),
            dma((SECTIONS,)),
            dma((3,)),
            dma((3,)),
        ],
        compiler_params=pltpu.CompilerParams(
            collective_id=0, has_side_effects=True, vmem_limit_bytes=55000 * 1024
        ),
        name="flow",
    )(sections_img, jnp.transpose(patch_anchor, (1, 2, 0)), missing, block_valid, jnp.asarray(tables()))
    return jnp.transpose(flow, (0, 1, 4, 2, 3))


def solution(mesh):
    placed = (P("sec", "xy", None), P(), P(None, "xy", "sec"), P("xy", "sec"))
    return jax.shard_map(
        functools.partial(body, mesh.shape["xy"]),
        mesh=mesh,
        in_specs=placed,
        out_specs=P(None, None, None, "xy", "sec"),
        check_vma=False,
    )
```
